128 devices in a mesh: dp: 2 (over z_lo), outer: 4 (over y), inner: 16 (over z_hi, x, core).
Axes of the slice: x: 4, y: 4, z: 4 (z_hi: 2, z_lo: 2; z = z_hi * 2 + z_lo), core: 2. Of those that a mesh axis runs over, the one named last changes fastest.
Arguments:
- query_gate: bfloat16 [65536, 256], P(('dp', 'outer', 'inner')), parts along dimension 0, may hold values from -6 to 6
- key_gate: bfloat16 [65536, 256], P(('dp', 'outer', 'inner')), parts along dimension 0, may hold values from -6 to 6
- value_seq: bfloat16 [65536, 256], P(('dp', 'outer', 'inner')), parts along dimension 0, may hold values from -6 to 6
- grad_output: bfloat16 [65536, 256], P(('dp', 'outer', 'inner')), parts along dimension 0, may hold values from -6 to 6
- filter_taps: float32 [32768, 256], P(('outer', 'inner')), may hold values from -2 to 2
Outputs:
- grad_query: bfloat16 [65536, 256], P(('dp', 'outer', 'inner')), parts along dimension 0
- grad_key: bfloat16 [65536, 256], P(('dp', 'outer', 'inner')), parts along dimension 0
- grad_value: bfloat16 [65536, 256], P(('dp', 'outer', 'inner')), parts along dimension 0
- grad_filter: float32 [65536, 256], P(('dp', 'outer', 'inner')), parts along dimension 0
The draws below stay inside these ranges and needn't reach their ends.
There are 2 independent parts, one for each index of `dp`. The reference program is written for one: setup_inputs(seed, part) draws one part's arguments, and reference() takes and returns one part's arrays. A program takes and returns all parts, laid end to end along the dimension named above; an argument that names none is the same for every part. Nothing has to cross between parts.
All inputs are finite; a program needn't handle non-finite values.
Results may differ from the reference program's by a relative error of at most 0.0025.
Values sent between devices are 32-bit elements; how exact they have to be, the bound alone decides.
No kernel may reach another device: no remote copies, remote signals or barrier semaphores. Data moves between devices by JAX's collectives and lax.ppermute only.
A program may use at most 128 MiB of HBM per device.

```python
import jax
import jax.numpy as jnp

C = 256
SEQ = 32768


def draw_filter_taps(key, part):
    key = jax.random.fold_in(key, 11)
    key_rate, key_noise = jax.random.split(key)
    spread = jax.random.uniform(key_rate, (1, C), jnp.float32)
    places = jnp.arange(SEQ, dtype=jnp.float32)[:, None]
    rates = jnp.exp(jnp.log(0.5 / SEQ) + spread * jnp.log(0.1 * SEQ))
    noise = jnp.clip(jax.random.normal(key_noise, (SEQ, C), jnp.float32), -4.0, 4.0)
    floor = 0.2
    envelope = jnp.sqrt(2.0 * rates) * jnp.exp(-rates * places) + floor * SEQ ** (-0.5)
    return noise * envelope


def block_levels(key, dims, shards, low, high):
    factor_of, own = 1.0, jax.random.fold_in(key, 6)
    for dim, shards_of in shards:
        draws = jnp.exp(jax.random.uniform(jax.random.fold_in(own, dim), (shards_of,), jnp.float32, low / len(shards), high / len(shards)))
        factor_of = factor_of * jnp.repeat(draws, dims[dim] // shards_of).reshape([-1 if axis == dim else 1 for axis in range(len(dims))])
    return factor_of


def centred(rng, dims, scale, reach, pieces=(), kind=jnp.bfloat16):
    values = scale * jax.random.normal(rng, dims, jnp.float32)
    if pieces:
        values = values * block_levels(rng, dims, pieces, -0.22, 0.18)
    return jnp.clip(values, -reach, reach).astype(kind)


def setup_inputs(seed: int = 0, part: int = 0) -> dict:
    streams_of = jax.random.split(jax.random.key(seed), 6)
    part_splits = jax.random.split(jax.random.fold_in(streams_of[5], part), 6)
    return {
        "query_gate": centred(part_splits[0], (SEQ, C), 1.0, 6.0, ((0, 64),)),
        "key_gate": centred(part_splits[1], (SEQ, C), 1.0, 6.0, ((0, 64),)),
        "value_seq": centred(part_splits[2], (SEQ, C), 1.0, 6.0, ((0, 64),)),
        "grad_output": centred(part_splits[3], (SEQ, C), 1.0, 6.0, ((0, 64),)),
        "filter_taps": draw_filter_taps(jax.random.fold_in(streams_of[5], 71), part),
    }


def reference(query_gate, key_gate, value_seq, grad_output, filter_taps):
    mixed_in = key_gate.astype(jnp.float32) * value_seq.astype(jnp.float32)
    grad_mix = grad_output.astype(jnp.float32) * query_gate.astype(jnp.float32)
    length = 2 * SEQ
    spec_mixed = jnp.fft.rfft(mixed_in, n=length, axis=0)
    spec_grad = jnp.fft.rfft(grad_mix, n=length, axis=0)
    spec_taps = jnp.fft.rfft(filter_taps, n=length, axis=0)
    convolved = jnp.fft.irfft(spec_taps * spec_mixed, n=length, axis=0)[:SEQ]
    correlated = jnp.fft.irfft(jnp.conj(spec_taps) * spec_grad, n=length, axis=0)[:SEQ]
    filter_grad = jnp.fft.irfft(jnp.conj(spec_mixed) * spec_grad, n=length, axis=0)[:SEQ]
    grad_query = (grad_output.astype(jnp.float32) * convolved).astype(jnp.bfloat16)
    grad_key = (correlated * value_seq.astype(jnp.float32)).astype(jnp.bfloat16)
    grad_value = (correlated * key_gate.astype(jnp.float32)).astype(jnp.bfloat16)
    grad_filter = (filter_grad * (1.0 / SEQ ** 0.5)).astype(jnp.float32)
    return grad_query, grad_key, grad_value, grad_filter
```

```python
import functools
import math

import jax
import jax.numpy as jnp
import numpy as np
from jax import lax
from jax.experimental import pallas as pl
from jax.experimental.pallas import tpu as pltpu
from jax.sharding import PartitionSpec as P

AXES = ("outer", "inner")
LANES = 128
SIGNALS = 3


def split_table(table):
    table = np.asarray(table, np.float32)
    high = table.astype(jnp.bfloat16)
    low = (table - high.astype(np.float32)).astype(jnp.bfloat16)
    return high, low


def tables(groups, width):
    pieces = width // LANES
    n1 = groups * pieces
    length = n1 * LANES
    order = (np.arange(groups)[None, :] * pieces + np.arange(pieces)[:, None]).reshape(-1)
    k1 = np.arange(n1) + 0.25
    turn = (k1[:, None] * order[None, :]) * (2.0 * math.pi / n1)
    outer = np.concatenate([np.cos(turn), -np.sin(turn)], axis=0)
    back_outer = np.concatenate([np.cos(turn.T), -np.sin(turn.T)], axis=1) / length
    twist = k1[:, None] * np.arange(LANES)[None, :] * (2.0 * math.pi / length)
    lane = np.arange(LANES)
    spin = lane[:, None] * lane[None, :] * (2.0 * math.pi / LANES)
    cos, sin = np.cos(spin), np.sin(spin)
    inner = np.block([[cos, -sin], [sin, cos]])
    back_inner = np.block([[cos, sin], [-sin, cos]])
    return (
        split_table(outer),
        split_table(inner),
        split_table(back_outer),
        split_table(back_inner),
        np.cos(twist).astype(np.float32),
        np.sin(twist).astype(np.float32),
    )


def split(value):
    high = value.astype(jnp.bfloat16)
    low = (value - high.astype(jnp.float32)).astype(jnp.bfloat16)
    return high, low


def dot3(left, right):
    dot = functools.partial(jnp.dot, preferred_element_type=jnp.float32)
    return dot(left[0], right[0]) + (dot(left[0], right[1]) + dot(left[1], right[0]))


def pack_kernel(groups, key_ref, value_ref, grad_ref, query_ref, taps_ref, out_ref):
    rows, channels = key_ref.shape
    pieces, per = rows // LANES, channels // groups
    slab = SIGNALS * per * pieces
    for piece in range(pieces):
        span = slice(piece * LANES, (piece + 1) * LANES)
        mixed = key_ref[span, :].astype(jnp.float32) * value_ref[span, :].astype(jnp.float32)
        grad = grad_ref[span, :].astype(jnp.float32) * query_ref[span, :].astype(jnp.float32)
        for s, signal in enumerate((mixed, grad, taps_ref[span, :])):
            turned = signal.T
            for c in range(per):
                row = (s * per + c) * pieces + piece
                out_ref[pl.ds(row, groups, stride=slab), :] = turned[c * groups : (c + 1) * groups, :]


def unpack_kernel(groups, in_ref, key_ref, value_ref, grad_ref, gq_ref, gk_ref, gv_ref, gf_ref):
    rows, channels = key_ref.shape
    pieces, per = rows // LANES, channels // groups
    slab = SIGNALS * per * pieces
    scale = 1.0 / math.sqrt(groups * rows)

    def signal(s, piece):
        parts = [
            in_ref[pl.ds((s * per + c) * pieces + piece, groups, stride=slab), :] for c in range(per)
        ]
        return jnp.concatenate(parts, axis=0).T

    for piece in range(pieces):
        span = slice(piece * LANES, (piece + 1) * LANES)
        gq_ref[span, :] = (grad_ref[span, :].astype(jnp.float32) * signal(0, piece)).astype(gq_ref.dtype)
        corr = signal(1, piece)
        gk_ref[span, :] = (corr * value_ref[span, :].astype(jnp.float32)).astype(gk_ref.dtype)
        gv_ref[span, :] = (corr * key_ref[span, :].astype(jnp.float32)).astype(gv_ref.dtype)
        gf_ref[span, :] = signal(2, piece) * scale


def convolve_kernel(
    groups, per, in_ref, outer_hi, outer_lo, inner_hi, inner_lo,
    back_outer_hi, back_outer_lo, back_inner_hi, back_inner_lo, cos_ref, sin_ref, out_ref,
):
    n1 = cos_ref.shape[0]
    pieces = n1 // groups
    slab = SIGNALS * per * pieces
    outer = (outer_hi[...], outer_lo[...])
    inner = (inner_hi[...], inner_lo[...])
    back_outer = (back_outer_hi[...], back_outer_lo[...])
    back_inner = (back_inner_hi[...], back_inner_lo[...])

    def load(s, c):
        parts = [
            in_ref[pl.ds((s * per + c) * pieces + piece, groups, stride=slab), :]
            for piece in range(pieces)
        ]
        return jnp.concatenate(parts, axis=0)

    def forward(s, c):
        pair = jnp.concatenate([load(s, c), load(s, c + 1)], axis=1)
        mixed = dot3(outer, split(pair))
        spectra = []
        for half in range(2):
            lanes = slice(half * LANES, (half + 1) * LANES)
            re, im = mixed[:n1, lanes], mixed[n1:, lanes]
            cos, sin = cos_ref[...], sin_ref[...]
            turned = jnp.concatenate([re * cos + im * sin, im * cos - re * sin], axis=1)
            done = dot3(split(turned), inner)
            spectra.append((done[:, :LANES], done[:, LANES:]))
        return spectra

    def product(left, right, sign):
        left_re, left_im = left[0], sign * left[1]
        re = left_re * right[0] - left_im * right[1]
        im = left_re * right[1] + left_im * right[0]
        return jnp.concatenate([re, im], axis=1)

    def inverse(s, c, spectra):
        columns = []
        for spectrum in spectra:
            done = dot3(split(spectrum), back_inner)
            re, im = done[:, :LANES], done[:, LANES:]
            cos, sin = cos_ref[...], sin_ref[...]
            columns.append(jnp.concatenate([re * cos - im * sin, re * sin + im * cos], axis=0))
        pair = dot3(back_outer, split(jnp.concatenate(columns, axis=1)))
        for half in range(2):
            for piece in range(pieces):
                row = (s * per + c + half) * pieces + piece
                block = pair[piece * groups : (piece + 1) * groups, half * LANES : (half + 1) * LANES]
                out_ref[pl.ds(row, groups, stride=slab), :] = block

    for c in range(0, per, 2):
        mixed, grad, taps = forward(0, c), forward(1, c), forward(2, c)
        inverse(0, c, [product(t, m, 1.0) for t, m in zip(taps, mixed)])
        inverse(1, c, [product(t, g, -1.0) for t, g in zip(taps, grad)])
        inverse(2, c, [product(m, g, -1.0) for m, g in zip(mixed, grad)])


def params(size):
    return pltpu.CompilerParams(vmem_limit_bytes=size << 20)


def exchange(slabs, groups):
    slabs = slabs.reshape(groups, -1, LANES)
    slabs = lax.all_to_all(slabs, AXES, split_axis=0, concat_axis=0, tiled=True)
    return slabs.reshape(-1, LANES)


def per_device(query_gate, key_gate, value_seq, grad_output, filter_taps):
    groups = lax.axis_size(AXES)
    rows, channels = query_gate.shape
    per = channels // groups
    flat = jax.ShapeDtypeStruct((SIGNALS * channels * rows // LANES, LANES), jnp.float32)
    outer, inner, back_outer, back_inner, cos, sin = tables(groups, rows)

    packed = pl.pallas_call(
        functools.partial(pack_kernel, groups), out_shape=flat, compiler_params=params(32), name="pack"
    )(key_gate, value_seq, grad_output, query_gate, filter_taps)
    received = exchange(packed, groups)
    results = pl.pallas_call(
        functools.partial(convolve_kernel, groups, per), out_shape=flat, compiler_params=params(48), name="convolve"
    )(received, *outer, *inner, *back_outer, *back_inner, cos, sin)
    returned = exchange(results, groups)
    narrow = jax.ShapeDtypeStruct((rows, channels), jnp.bfloat16)
    wide = jax.ShapeDtypeStruct((rows, channels), jnp.float32)
    return pl.pallas_call(
        functools.partial(unpack_kernel, groups),
        out_shape=(narrow, narrow, narrow, wide),
        compiler_params=params(32),
        name="unpack",
    )(returned, key_gate, value_seq, grad_output)


def solution(mesh):
    split_rows = P(("dp",) + AXES, None)
    return jax.shard_map(
        per_device,
        mesh=mesh,
        in_specs=(split_rows, split_rows, split_rows, split_rows, P(AXES, None)),
        out_specs=(split_rows, split_rows, split_rows, split_rows),
        check_vma=False,
    )
```

```python
import functools
import math

import jax
import jax.numpy as jnp
import numpy as np
from jax import lax
from jax.experimental import pallas as pl
from jax.experimental.pallas import tpu as pltpu
from jax.sharding import PartitionSpec as P

BLOCK_AXES = ("outer", "inner")
ALL_AXES = ("dp",) + BLOCK_AXES
LANES = 128


def split_table(table):
    table = np.asarray(table, np.float32)
    high = table.astype(jnp.bfloat16)
    low = (table - high.astype(np.float32)).astype(jnp.bfloat16)
    return high, low


def tables(groups, width):
    pieces = width // LANES
    n1 = groups * pieces
    length = n1 * LANES
    order = (np.arange(groups)[None, :] * pieces + np.arange(pieces)[:, None]).reshape(-1)
    k1 = np.arange(n1) + 0.25
    turn = (k1[:, None] * order[None, :]) * (2.0 * math.pi / n1)
    outer = np.concatenate([np.cos(turn), -np.sin(turn)], axis=0)
    back_outer = np.concatenate([np.cos(turn.T), -np.sin(turn.T)], axis=1) / length
    twist = k1[:, None] * np.arange(LANES)[None, :] * (2.0 * math.pi / length)
    lane = np.arange(LANES)
    spin = lane[:, None] * lane[None, :] * (2.0 * math.pi / LANES)
    cos, sin = np.cos(spin), np.sin(spin)
    inner = np.block([[cos, -sin], [sin, cos]])
    back_inner = np.block([[cos, sin], [-sin, cos]])
    return (
        split_table(outer),
        split_table(inner),
        split_table(back_outer),
        split_table(back_inner),
        np.cos(twist).astype(np.float32),
        np.sin(twist).astype(np.float32),
    )


def split(value):
    high = value.astype(jnp.bfloat16)
    low = (value - high.astype(jnp.float32)).astype(jnp.bfloat16)
    return high, low


def dot3(left, right):
    dot = functools.partial(jnp.dot, preferred_element_type=jnp.float32)
    return dot(left[0], right[0]) + (dot(left[0], right[1]) + dot(left[1], right[0]))


def pack_kernel(
    parts, devices, key_hbm, value_hbm, grad_hbm, query_hbm, taps_hbm, out_ref, key, value, grad, query, taps, sems
):
    rows, channels = key.shape
    pieces, per = rows // LANES, channels // devices
    taps_pieces = pieces // parts
    slab = per * (2 * pieces + taps_pieces)
    start = lax.axis_index("dp") * (taps_pieces * LANES)

    def copies(piece):
        span = pl.ds(piece * LANES, LANES)
        moves = [
            pltpu.make_async_copy(src.at[span, :], dst.at[span, :], sems.at[n, piece])
            for n, (src, dst) in enumerate(
                ((key_hbm, key), (value_hbm, value), (grad_hbm, grad), (query_hbm, query))
            )
        ]
        if piece < taps_pieces:
            here = pl.ds(pl.multiple_of(start + piece * LANES, LANES), LANES)
            moves.append(pltpu.make_async_copy(taps_hbm.at[here, :], taps.at[span, :], sems.at[4, piece]))
        return moves

    def put(signal, first, count, piece):
        turned = signal.T
        for c in range(per):
            row = first + c * count + piece
            out_ref[pl.ds(row, devices, stride=slab), :] = turned[c * devices : (c + 1) * devices, :]

    moves = [copies(piece) for piece in range(pieces)]
    for group in moves:
        for move in group:
            move.start()
    for piece in range(pieces):
        for move in moves[piece]:
            move.wait()
        span = slice(piece * LANES, (piece + 1) * LANES)
        put(key[span, :].astype(jnp.float32) * value[span, :].astype(jnp.float32), 0, pieces, piece)
        put(grad[span, :].astype(jnp.float32) * query[span, :].astype(jnp.float32), per * pieces, pieces, piece)
        if piece < taps_pieces:
            put(taps[span, :], 2 * per * pieces, taps_pieces, piece)


def unpack_kernel(
    devices, scale, in_ref, key_ref, value_ref, grad_ref, gq_hbm, gk_hbm, gv_hbm, gf_hbm, gq, gk, gv, gf, sems
):
    rows, channels = key_ref.shape
    pieces, per = rows // LANES, channels // devices
    slab = 3 * per * pieces

    def signal(s, piece):
        parts = [
            in_ref[pl.ds((s * per + c) * pieces + piece, devices, stride=slab), :] for c in range(per)
        ]
        return jnp.concatenate(parts, axis=0).T

    moves = []
    for piece in range(pieces):
        span = slice(piece * LANES, (piece + 1) * LANES)
        gq[span, :] = (grad_ref[span, :].astype(jnp.float32) * signal(0, piece)).astype(gq.dtype)
        corr = signal(1, piece)
        gk[span, :] = (corr * value_ref[span, :].astype(jnp.float32)).astype(gk.dtype)
        gv[span, :] = (corr * key_ref[span, :].astype(jnp.float32)).astype(gv.dtype)
        gf[span, :] = signal(2, piece) * scale
        for n, (src, dst) in enumerate(((gq, gq_hbm), (gk, gk_hbm), (gv, gv_hbm), (gf, gf_hbm))):
            here = pl.ds(piece * LANES, LANES)
            moves.append(pltpu.make_async_copy(src.at[here, :], dst.at[here, :], sems.at[n, piece]))
            moves[-1].start()
    for move in moves:
        move.wait()


def convolve_kernel(
    parts, blocks, per, in_ref, outer_hi, outer_lo, inner_hi, inner_lo,
    back_outer_hi, back_outer_lo, back_inner_hi, back_inner_lo, cos_ref, sin_ref, out_ref,
):
    n1 = cos_ref.shape[0]
    pieces = n1 // blocks
    taps_pieces = pieces // parts
    slab_in = per * (2 * pieces + taps_pieces)
    slab_out = 3 * per * pieces
    outer = (outer_hi[...], outer_lo[...])
    inner = (inner_hi[...], inner_lo[...])
    back_outer = (back_outer_hi[...], back_outer_lo[...])
    back_inner = (back_inner_hi[...], back_inner_lo[...])

    def load(row, part):
        return in_ref[pl.ds(part * blocks * slab_in + row, blocks, stride=slab_in), :]

    def load_signal(s, c, part):
        return jnp.concatenate([load((s * per + c) * pieces + piece, part) for piece in range(pieces)], axis=0)

    def load_taps(c):
        first = (2 * pieces * per) + c * taps_pieces
        return jnp.concatenate(
            [load(first + piece % taps_pieces, piece // taps_pieces) for piece in range(pieces)], axis=0
        )

    def forward(signals):
        mixed = dot3(outer, split(jnp.concatenate(signals, axis=1)))
        spectra = []
        for n in range(len(signals)):
            lanes = slice(n * LANES, (n + 1) * LANES)
            re, im = mixed[:n1, lanes], mixed[n1:, lanes]
            cos, sin = cos_ref[...], sin_ref[...]
            turned = jnp.concatenate([re * cos + im * sin, im * cos - re * sin], axis=1)
            done = dot3(split(turned), inner)
            spectra.append((done[:, :LANES], done[:, LANES:]))
        return spectra

    def product(left, right, sign):
        left_re, left_im = left[0], sign * left[1]
        re = left_re * right[0] - left_im * right[1]
        im = left_re * right[1] + left_im * right[0]
        return jnp.concatenate([re, im], axis=1)

    def inverse(s, c, spectra):
        columns = []
        for spectrum in spectra:
            done = dot3(split(spectrum), back_inner)
            re, im = done[:, :LANES], done[:, LANES:]
            cos, sin = cos_ref[...], sin_ref[...]
            columns.append(jnp.concatenate([re * cos - im * sin, re * sin + im * cos], axis=0))
        signals = dot3(back_outer, split(jnp.concatenate(columns, axis=1)))
        for part in range(len(spectra)):
            for piece in range(pieces):
                row = part * blocks * slab_out + (s * per + c) * pieces + piece
                block = signals[piece * blocks : (piece + 1) * blocks, part * LANES : (part + 1) * LANES]
                out_ref[pl.ds(row, blocks, stride=slab_out), :] = block

    taps = forward([load_taps(c) for c in range(per)])
    for c in range(per):
        mixed = forward([load_signal(0, c, part) for part in range(parts)])
        grad = forward([load_signal(1, c, part) for part in range(parts)])
        inverse(0, c, [product(taps[c], m, 1.0) for m in mixed])
        inverse(1, c, [product(taps[c], g, -1.0) for g in grad])
        inverse(2, c, [product(m, g, -1.0) for m, g in zip(mixed, grad)])


def params(size):
    return pltpu.CompilerParams(vmem_limit_bytes=size << 20)


def exchange(slabs, devices):
    slabs = slabs.reshape(devices, -1, 4, LANES)
    slabs = lax.all_to_all(slabs, ALL_AXES, split_axis=0, concat_axis=0, tiled=True)
    return slabs.reshape(-1, LANES)


def per_device(query_gate, key_gate, value_seq, grad_output, filter_taps):
    parts = lax.axis_size("dp")
    blocks = lax.axis_size(BLOCK_AXES)
    devices = parts * blocks
    rows, channels = query_gate.shape
    per = channels // devices
    pieces = rows // LANES
    outer, inner, back_outer, back_inner, cos, sin = tables(blocks, rows)
    in_hbm = pl.BlockSpec(memory_space=pltpu.HBM)
    in_vmem = pl.BlockSpec(memory_space=pltpu.VMEM)
    gate = pltpu.VMEM((rows, channels), jnp.bfloat16)

    packed = pl.pallas_call(
        functools.partial(pack_kernel, parts, devices),
        out_shape=jax.ShapeDtypeStruct((channels * (2 * pieces + pieces // parts), LANES), jnp.float32),
        in_specs=[in_hbm] * 5,
        out_specs=in_vmem,
        scratch_shapes=[gate] * 4
        + [pltpu.VMEM((rows // parts, channels), jnp.float32), pltpu.SemaphoreType.DMA((5, pieces))],
        compiler_params=params(62),
        name="pack",
    )(key_gate, value_seq, grad_output, query_gate, filter_taps)
    received = exchange(packed, devices)
    results = pl.pallas_call(
        functools.partial(convolve_kernel, parts, blocks, per),
        out_shape=jax.ShapeDtypeStruct((3 * channels * pieces, LANES), jnp.float32),
        compiler_params=params(48),
        name="convolve",
    )(received, *outer, *inner, *back_outer, *back_inner, cos, sin)
    returned = exchange(results, devices)
    narrow = jax.ShapeDtypeStruct((rows, channels), jnp.bfloat16)
    wide = jax.ShapeDtypeStruct((rows, channels), jnp.float32)
    return pl.pallas_call(
        functools.partial(unpack_kernel, devices, 1.0 / math.sqrt(blocks * rows)),
        out_shape=(narrow, narrow, narrow, wide),
        in_specs=[in_vmem] * 4,
        out_specs=[in_hbm] * 4,
        scratch_shapes=[gate] * 3
        + [pltpu.VMEM((rows, channels), jnp.float32), pltpu.SemaphoreType.DMA((4, pieces))],
        compiler_params=params(32),
        name="unpack",
    )(returned, key_gate, value_seq, grad_output)


def solution(mesh):
    split_rows = P(ALL_AXES, None)
    return jax.shard_map(
        per_device,
        mesh=mesh,
        in_specs=(split_rows, split_rows, split_rows, split_rows, P(BLOCK_AXES, None)),
        out_specs=(split_rows, split_rows, split_rows, split_rows),
        check_vma=False,
    )
```

```python
import functools
import math

import jax
import jax.numpy as jnp
import numpy as np
from jax import lax
from jax.experimental import pallas as pl
from jax.experimental.pallas import tpu as pltpu
from jax.sharding import PartitionSpec as P

BLOCK_AXES = ("outer", "inner")
ALL_AXES = ("dp",) + BLOCK_AXES
LANES = 128


def split_table(table):
    table = np.asarray(table, np.float32)
    high = table.astype(jnp.bfloat16)
    low = (table - high.astype(np.float32)).astype(jnp.bfloat16)
    return high, low


def tables(groups, width):
    pieces = width // LANES
    n1 = groups * pieces
    length = n1 * LANES
    order = (np.arange(groups)[None, :] * pieces + np.arange(pieces)[:, None]).reshape(-1)
    k1 = np.arange(n1) + 0.25
    turn = (k1[:, None] * order[None, :]) * (2.0 * math.pi / n1)
    outer = np.concatenate([np.cos(turn), -np.sin(turn)], axis=0)
    back_outer = np.concatenate([np.cos(turn.T), -np.sin(turn.T)], axis=1) / length
    twist = k1[:, None] * np.arange(LANES)[None, :] * (2.0 * math.pi / length)
    lane = np.arange(LANES)
    spin = lane[:, None] * lane[None, :] * (2.0 * math.pi / LANES)
    cos, sin = np.cos(spin), np.sin(spin)
    inner = np.block([[cos, -sin], [sin, cos]])
    back_inner = np.block([[cos, sin], [-sin, cos]])
    return (
        split_table(outer),
        split_table(inner),
        split_table(back_outer),
        split_table(back_inner),
        np.cos(twist).astype(np.float32),
        np.sin(twist).astype(np.float32),
    )


def split(value):
    high = value.astype(jnp.bfloat16)
    low = (value - high.astype(jnp.float32)).astype(jnp.bfloat16)
    return high, low


def dot3(left, right):
    dot = functools.partial(jnp.dot, preferred_element_type=jnp.float32)
    return dot(left[0], right[0]) + (dot(left[0], right[1]) + dot(left[1], right[0]))


def pack_kernel(
    parts, devices, key_hbm, value_hbm, grad_hbm, query_hbm, taps_hbm, out_ref, key, value, grad, query, taps, sems
):
    rows, channels = key.shape
    pieces, per = rows // LANES, channels // devices
    taps_pieces = pieces // parts
    slab = per * (2 * pieces + taps_pieces)
    start = lax.axis_index("dp") * (taps_pieces * LANES)

    def copies(piece):
        span = pl.ds(piece * LANES, LANES)
        moves = [
            pltpu.make_async_copy(src.at[span, :], dst.at[span, :], sems.at[n, piece])
            for n, (src, dst) in enumerate(
                ((key_hbm, key), (value_hbm, value), (grad_hbm, grad), (query_hbm, query))
            )
        ]
        if piece < taps_pieces:
            here = pl.ds(pl.multiple_of(start + piece * LANES, LANES), LANES)
            moves.append(pltpu.make_async_copy(taps_hbm.at[here, :], taps.at[span, :], sems.at[4, piece]))
        return moves

    def put(signal, first, count, piece):
        turned = signal.T
        for c in range(per):
            row = first + c * count + piece
            out_ref[pl.ds(row, devices, stride=slab), :] = turned[c * devices : (c + 1) * devices, :]

    moves = [copies(piece) for piece in range(pieces)]
    for group in moves:
        for move in group:
            move.start()
    for piece in range(pieces):
        for move in moves[piece]:
            move.wait()
        span = slice(piece * LANES, (piece + 1) * LANES)
        put(key[span, :].astype(jnp.float32) * value[span, :].astype(jnp.float32), 0, pieces, piece)
        put(grad[span, :].astype(jnp.float32) * query[span, :].astype(jnp.float32), per * pieces, pieces, piece)
        if piece < taps_pieces:
            put(taps[span, :], 2 * per * pieces, taps_pieces, piece)


def unpack_kernel(
    devices, scale, in_ref, key_ref, value_ref, grad_ref, gq_hbm, gk_hbm, gv_hbm, gf_hbm, gq, gk, gv, gf, sems
):
    rows, channels = key_ref.shape
    pieces, per = rows // LANES, channels // devices
    slab = 3 * per * pieces

    def signal(s, piece):
        parts = [
            in_ref[pl.ds((s * per + c) * pieces + piece, devices, stride=slab), :] for c in range(per)
        ]
        return jnp.concatenate(parts, axis=0).T

    moves = []
    for piece in range(pieces):
        span = slice(piece * LANES, (piece + 1) * LANES)
        gq[span, :] = (grad_ref[span, :].astype(jnp.float32) * signal(0, piece)).astype(gq.dtype)
        corr = signal(1, piece)
        gk[span, :] = (corr * value_ref[span, :].astype(jnp.float32)).astype(gk.dtype)
        gv[span, :] = (corr * key_ref[span, :].astype(jnp.float32)).astype(gv.dtype)
        gf[span, :] = signal(2, piece) * scale
        for n, (src, dst) in enumerate(((gq, gq_hbm), (gk, gk_hbm), (gv, gv_hbm), (gf, gf_hbm))):
            here = pl.ds(piece * LANES, LANES)
            moves.append(pltpu.make_async_copy(src.at[here, :], dst.at[here, :], sems.at[n, piece]))
            moves[-1].start()
    for move in moves:
        move.wait()


def convolve_kernel(
    parts, blocks, per, in_ref, outer_hi, outer_lo, inner_hi, inner_lo,
    back_outer_hi, back_outer_lo, back_inner_hi, back_inner_lo, cos_ref, sin_ref, out_ref,
):
    n1 = cos_ref.shape[0]
    pieces = n1 // blocks
    taps_pieces = pieces // parts
    slab_in = per * (2 * pieces + taps_pieces)
    slab_out = 3 * per * pieces
    outer = (outer_hi[...], outer_lo[...])
    inner = (inner_hi[...], inner_lo[...])
    back_outer = (back_outer_hi[...], back_outer_lo[...])
    back_inner = (back_inner_hi[...], back_inner_lo[...])

    def load(row, part):
        return in_ref[pl.ds(part * blocks * slab_in + row, blocks, stride=slab_in), :]

    def load_signal(s, c, part):
        return jnp.concatenate([load((s * per + c) * pieces + piece, part) for piece in range(pieces)], axis=0)

    def load_taps(c):
        first = (2 * pieces * per) + c * taps_pieces
        return jnp.concatenate(
            [load(first + piece % taps_pieces, piece // taps_pieces) for piece in range(pieces)], axis=0
        )

    def outer_step(signals):
        mixed = dot3(outer, split(jnp.concatenate(signals, axis=1)))
        turned = []
        for n in range(len(signals)):
            lanes = slice(n * LANES, (n + 1) * LANES)
            re, im = mixed[:n1, lanes], mixed[n1:, lanes]
            cos, sin = cos_ref[...], sin_ref[...]
            turned.append(jnp.concatenate([re * cos + im * sin, im * cos - re * sin], axis=1))
        return split(jnp.concatenate(turned, axis=0))

    def inner_step(turned):
        return dot3(turned, inner)

    def product(left, right, sign):
        left_re, left_im = left[:, :LANES], sign * left[:, LANES:]
        right_re, right_im = right[:, :LANES], right[:, LANES:]
        re = left_re * right_re - left_im * right_im
        im = left_re * right_im + left_im * right_re
        return jnp.concatenate([re, im], axis=1)

    def back_inner_step(products):
        done = dot3(split(products), back_inner)
        columns = []
        for n in range(parts):
            re, im = done[n * n1 : (n + 1) * n1, :LANES], done[n * n1 : (n + 1) * n1, LANES:]
            cos, sin = cos_ref[...], sin_ref[...]
            columns.append(jnp.concatenate([re * cos - im * sin, re * sin + im * cos], axis=0))
        return jnp.concatenate(columns, axis=1)

    def back_outer_step(s, c, columns):
        signals = dot3(back_outer, split(columns))
        for part in range(parts):
            for piece in range(pieces):
                row = part * blocks * slab_out + (s * per + c) * pieces + piece
                block = signals[piece * blocks : (piece + 1) * blocks, part * LANES : (part + 1) * LANES]
                out_ref[pl.ds(row, blocks, stride=slab_out), :] = block

    def signal(s, c):
        return [load_signal(s, c, part) for part in range(parts)]

    def many(one):
        return jnp.concatenate([one] * parts, axis=0)

    t = outer_step([load_taps(c) for c in range(per)])
    m0 = outer_step(signal(0, 0))
    t = inner_step(t)
    taps = [many(t[c * n1 : (c + 1) * n1]) for c in range(per)]
    g0 = outer_step(signal(1, 0))
    m0 = inner_step(m0)
    m1 = outer_step(signal(0, 1))
    conv0 = back_inner_step(product(taps[0], m0, 1.0))
    g0 = inner_step(g0)
    g1 = outer_step(signal(1, 1))
    back_outer_step(0, 0, conv0)
    corr0 = back_inner_step(product(taps[0], g0, -1.0))
    m1 = inner_step(m1)
    back_outer_step(1, 0, corr0)
    cross0 = back_inner_step(product(m0, g0, -1.0))
    g1 = inner_step(g1)
    back_outer_step(2, 0, cross0)
    conv1 = back_inner_step(product(taps[1], m1, 1.0))
    corr1 = back_inner_step(product(taps[1], g1, -1.0))
    back_outer_step(0, 1, conv1)
    cross1 = back_inner_step(product(m1, g1, -1.0))
    back_outer_step(1, 1, corr1)
    back_outer_step(2, 1, cross1)


def params(size):
    return pltpu.CompilerParams(vmem_limit_bytes=size << 20)


def exchange(slabs, devices):
    slabs = slabs.reshape(devices, -1, 4, LANES)
    slabs = lax.all_to_all(slabs, ALL_AXES, split_axis=0, concat_axis=0, tiled=True)
    return slabs.reshape(-1, LANES)


def per_device(query_gate, key_gate, value_seq, grad_output, filter_taps):
    parts = lax.axis_size("dp")
    blocks = lax.axis_size(BLOCK_AXES)
    devices = parts * blocks
    rows, channels = query_gate.shape
    per = channels // devices
    pieces = rows // LANES
    outer, inner, back_outer, back_inner, cos, sin = tables(blocks, rows)
    in_hbm = pl.BlockSpec(memory_space=pltpu.HBM)
    in_vmem = pl.BlockSpec(memory_space=pltpu.VMEM)
    gate = pltpu.VMEM((rows, channels), jnp.bfloat16)

    packed = pl.pallas_call(
        functools.partial(pack_kernel, parts, devices),
        out_shape=jax.ShapeDtypeStruct((channels * (2 * pieces + pieces // parts), LANES), jnp.float32),
        in_specs=[in_hbm] * 5,
        out_specs=in_vmem,
        scratch_shapes=[gate] * 4
        + [pltpu.VMEM((rows // parts, channels), jnp.float32), pltpu.SemaphoreType.DMA((5, pieces))],
        compiler_params=params(32),
        name="pack",
    )(*(pltpu.with_memory_space_constraint(x, pltpu.HBM) for x in (key_gate, value_seq, grad_output, query_gate, filter_taps)))
    received = exchange(packed, devices)
    results = pl.pallas_call(
        functools.partial(convolve_kernel, parts, blocks, per),
        out_shape=jax.ShapeDtypeStruct((3 * channels * pieces, LANES), jnp.float32),
        compiler_params=params(48),
        name="convolve",
    )(received, *outer, *inner, *back_outer, *back_inner, cos, sin)
    returned = exchange(results, devices)
    narrow = jax.ShapeDtypeStruct((rows, channels), jnp.bfloat16)
    wide = jax.ShapeDtypeStruct((rows, channels), jnp.float32)
    return pl.pallas_call(
        functools.partial(unpack_kernel, devices, 1.0 / math.sqrt(blocks * rows)),
        out_shape=(narrow, narrow, narrow, wide),
        in_specs=[in_vmem] * 4,
        out_specs=[in_hbm] * 4,
        scratch_shapes=[gate] * 3
        + [pltpu.VMEM((rows, channels), jnp.float32), pltpu.SemaphoreType.DMA((4, pieces))],
        compiler_params=params(32),
        name="unpack",
    )(returned, key_gate, value_seq, grad_output)


def solution(mesh):
    split_rows = P(ALL_AXES, None)
    return jax.shard_map(
        per_device,
        mesh=mesh,
        in_specs=(split_rows, split_rows, split_rows, split_rows, P(BLOCK_AXES, None)),
        out_specs=(split_rows, split_rows, split_rows, split_rows),
        check_vma=False,
    )
```

```python
import functools
import math

import jax
import jax.numpy as jnp
import numpy as np
from jax import lax
from jax.experimental import pallas as pl
from jax.experimental.pallas import tpu as pltpu
from jax.sharding import PartitionSpec as P

BLOCK_AXES = ("outer", "inner")
ALL_AXES = ("dp",) + BLOCK_AXES
LANES = 128


def split_table(table):
    table = np.asarray(table, np.float32)
    high = table.astype(jnp.bfloat16)
    low = (table - high.astype(np.float32)).astype(jnp.bfloat16)
    return high, low


def square_table(table):
    high, low = split_table(table)
    return np.block([[high, low], [high, np.zeros_like(low)]])


def tables(groups, width):
    pieces = width // LANES
    n1 = groups * pieces
    length = n1 * LANES
    order = (np.arange(groups)[None, :] * pieces + np.arange(pieces)[:, None]).reshape(-1)
    k1 = np.arange(n1) + 0.25
    turn = (k1[:, None] * order[None, :]) * (2.0 * math.pi / n1)
    outer = np.concatenate([np.cos(turn), -np.sin(turn)], axis=0)
    back_outer = np.concatenate([np.cos(turn.T), -np.sin(turn.T)], axis=1) / length
    twist = k1[:, None] * np.arange(LANES)[None, :] * (2.0 * math.pi / length)
    half = np.arange(LANES // 2)
    even = half[:, None] * half[None, :] * (4.0 * math.pi / LANES)
    odd = half[:, None] * (2 * half[None, :] + 1) * (2.0 * math.pi / LANES)
    inner_even = np.block([[np.cos(even), -np.sin(even)], [np.sin(even), np.cos(even)]])
    inner_odd = np.block([[np.cos(odd), -np.sin(odd)], [-np.sin(odd), -np.cos(odd)]])
    back_even = np.block([[np.cos(even.T), np.sin(even.T)], [-np.sin(even.T), np.cos(even.T)]])
    back_odd = np.block([[np.cos(odd.T), np.sin(odd.T)], [-np.sin(odd.T), np.cos(odd.T)]])
    back_high, back_low = split_table(back_outer)
    narrow = [
        *split_table(outer),
        *(half for whole in (back_high, back_low) for half in np.split(whole, 2, axis=1)),
        *(square_table(t) for t in (inner_even, inner_odd, back_even, back_odd)),
    ]
    return np.concatenate(narrow, axis=0), np.stack([np.cos(twist), np.sin(twist)]).astype(np.float32)


def split(value):
    high = value.astype(jnp.bfloat16)
    low = (value - high.astype(jnp.float32)).astype(jnp.bfloat16)
    return high, low


def dot3(left, right):
    wide = jnp.concatenate([left[0], left[1], left[0]], axis=1)
    tall = jnp.concatenate([right[0], right[0], right[1]], axis=0)
    return jnp.dot(wide, tall, preferred_element_type=jnp.float32)


def dot_square(value, table):
    sums = jnp.dot(jnp.concatenate(split(value), axis=1), table, preferred_element_type=jnp.float32)
    return sums[:, :LANES] + sums[:, LANES:]


def pack_kernel(
    parts, devices, key_hbm, value_hbm, grad_hbm, query_hbm, taps_hbm, out_ref, key, value, grad, query, taps, sems
):
    rows, channels = key.shape
    pieces, per = rows // LANES, channels // devices
    taps_rows = rows // parts
    taps_pieces = taps_rows // LANES
    slab = per * (2 * pieces + taps_pieces)
    start = pl.multiple_of(lax.axis_index("dp") * taps_rows, taps_rows)

    def put(signal, first, count, piece):
        turned = signal.T
        for c in range(per):
            row = first + c * count + piece
            out_ref[pl.ds(row, devices, stride=slab), :] = turned[c * devices : (c + 1) * devices, :]

    def put_product(left, right, first):
        for piece in range(pieces):
            span = slice(piece * LANES, (piece + 1) * LANES)
            put(left[span, :].astype(jnp.float32) * right[span, :].astype(jnp.float32), first, pieces, piece)

    sources = (key_hbm, value_hbm, taps_hbm.at[pl.ds(start, taps_rows), :], grad_hbm, query_hbm)
    targets = (key, value, taps, grad, query)
    moves = [pltpu.make_async_copy(src, dst, sems.at[n]) for n, (src, dst) in enumerate(zip(sources, targets))]
    for move in moves:
        move.start()
    moves[0].wait()
    moves[1].wait()
    put_product(key, value, 0)
    moves[2].wait()
    for piece in range(taps_pieces):
        put(taps[piece * LANES : (piece + 1) * LANES, :], 2 * per * pieces, taps_pieces, piece)
    moves[3].wait()
    moves[4].wait()
    put_product(grad, query, per * pieces)


def unpack_kernel(
    devices, scale, in_ref, key_ref, value_ref, grad_ref, gq_hbm, gk_hbm, gv_hbm, gf_hbm, gq, gk, gv, gf, sems
):
    rows, channels = key_ref.shape
    pieces, per = rows // LANES, channels // devices
    slab = 3 * per * pieces

    def signal(s, piece):
        parts = [
            in_ref[pl.ds((s * per + c) * pieces + piece, devices, stride=slab), :] for c in range(per)
        ]
        return jnp.concatenate(parts, axis=0).T

    moves = []
    for piece in range(pieces):
        span = slice(piece * LANES, (piece + 1) * LANES)
        gq[span, :] = (grad_ref[span, :].astype(jnp.float32) * signal(0, piece)).astype(gq.dtype)
        corr = signal(1, piece)
        gk[span, :] = (corr * value_ref[span, :].astype(jnp.float32)).astype(gk.dtype)
        gv[span, :] = (corr * key_ref[span, :].astype(jnp.float32)).astype(gv.dtype)
        gf[span, :] = signal(2, piece) * scale
        for n, (src, dst) in enumerate(((gq, gq_hbm), (gk, gk_hbm), (gv, gv_hbm), (gf, gf_hbm))):
            here = pl.ds(piece * LANES, LANES)
            moves.append(pltpu.make_async_copy(src.at[here, :], dst.at[here, :], sems.at[n, piece]))
            moves[-1].start()
    for move in moves:
        move.wait()


def convolve_kernel(parts, blocks, per, in_ref, tables_ref, twist_ref, out_ref):
    n1 = twist_ref.shape[1]
    pieces = n1 // blocks
    taps_pieces = pieces // parts
    slab_in = per * (2 * pieces + taps_pieces)
    slab_out = 3 * per * pieces
    square = 2 * LANES

    def table(start, rows):
        return tables_ref[start : start + rows, :]

    def wide_table(start):
        return jnp.concatenate([table(start, n1), table(start + n1, n1)], axis=1)

    outer = (table(0, 2 * n1), table(2 * n1, 2 * n1))
    back_outer = (wide_table(4 * n1), wide_table(6 * n1))
    even, odd, back_even, back_odd = (table(8 * n1 + n * square, square) for n in range(4))

    def first_half(left, right):
        lane = lax.broadcasted_iota(jnp.int32, left.shape, 1)
        return jnp.where(lane < LANES // 2, left, right)

    def swap(value):
        return pltpu.roll(value, LANES // 2, 1)

    def load(row, part):
        return in_ref[pl.ds(part * blocks * slab_in + row, blocks, stride=slab_in), :]

    def load_signal(s, c, part):
        return jnp.concatenate([load((s * per + c) * pieces + piece, part) for piece in range(pieces)], axis=0)

    def load_taps(c):
        first = (2 * pieces * per) + c * taps_pieces
        return jnp.concatenate(
            [load(first + piece % taps_pieces, piece // taps_pieces) for piece in range(pieces)], axis=0
        )

    def outer_step(signals):
        mixed = dot3(outer, split(jnp.concatenate(signals, axis=1)))
        ups, downs = [], []
        for n in range(len(signals)):
            lanes = slice(n * LANES, (n + 1) * LANES)
            re, im = mixed[:n1, lanes], mixed[n1:, lanes]
            cos, sin = twist_ref[0], twist_ref[1]
            re, im = re * cos + im * sin, im * cos - re * sin
            near, far = first_half(re, im), swap(first_half(im, re))
            ups.append(near + far)
            downs.append(near - far)
        return jnp.concatenate(ups, axis=0), jnp.concatenate(downs, axis=0)

    def inner_step(turned):
        spectra = (dot_square(turned[0], even), dot_square(turned[1], odd))
        return [(one, swap(one)) for one in spectra]

    def factors(spectra):
        return [(first_half(one, other), first_half(-other, one)) for one, other in spectra]

    def product(left, right):
        return [one * re + other * im for (one, other), (re, im) in zip(left, right)]

    def product_conjugate(left, right):
        return [one * re - other * im for (one, other), (re, im) in zip(left, right)]

    def back_inner_step(products):
        sums_even, sums_odd = dot_square(products[0], back_even), dot_square(products[1], back_odd)
        near, far = sums_even + sums_odd, sums_even - sums_odd
        turned = swap(first_half(far, near))
        res, ims = first_half(near, turned), first_half(turned, far)
        columns = []
        for n in range(parts):
            re, im = res[n * n1 : (n + 1) * n1], ims[n * n1 : (n + 1) * n1]
            cos, sin = twist_ref[0], twist_ref[1]
            columns.append(jnp.concatenate([re * cos - im * sin, re * sin + im * cos], axis=0))
        return jnp.concatenate(columns, axis=1)

    def back_outer_step(s, c, columns):
        signals = dot3(back_outer, split(columns))
        for part in range(parts):
            for piece in range(pieces):
                row = part * blocks * slab_out + (s * per + c) * pieces + piece
                block = signals[piece * blocks : (piece + 1) * blocks, part * LANES : (part + 1) * LANES]
                out_ref[pl.ds(row, blocks, stride=slab_out), :] = block

    def signal(s, c):
        return [load_signal(s, c, part) for part in range(parts)]

    def channel(pair, c):
        one = pair[c * n1 : (c + 1) * n1]
        return jnp.concatenate([one] * parts, axis=0)

    m0 = outer_step(signal(0, 0))
    g0 = outer_step(signal(1, 0))
    t = outer_step([load_taps(c) for c in range(per)])
    m0 = inner_step(m0)
    g0 = inner_step(g0)
    t = factors(inner_step(t))
    taps = [[tuple(channel(f, c) for f in half) for half in t] for c in range(per)]
    m1 = outer_step(signal(0, 1))
    g1 = outer_step(signal(1, 1))
    cross0 = back_inner_step(product_conjugate(g0, factors(m0)))
    conv0 = back_inner_step(product(m0, taps[0]))
    corr0 = back_inner_step(product_conjugate(g0, taps[0]))
    back_outer_step(2, 0, cross0)
    back_outer_step(0, 0, conv0)
    back_outer_step(1, 0, corr0)
    m1 = inner_step(m1)
    g1 = inner_step(g1)
    cross1 = back_inner_step(product_conjugate(g1, factors(m1)))
    conv1 = back_inner_step(product(m1, taps[1]))
    corr1 = back_inner_step(product_conjugate(g1, taps[1]))
    back_outer_step(2, 1, cross1)
    back_outer_step(0, 1, conv1)
    back_outer_step(1, 1, corr1)


def params(size):
    return pltpu.CompilerParams(vmem_limit_bytes=size << 20)


def exchange(slabs, devices):
    slabs = slabs.reshape(devices, -1, 4, LANES)
    slabs = lax.all_to_all(slabs, ALL_AXES, split_axis=0, concat_axis=0, tiled=True)
    return slabs.reshape(-1, LANES)


def per_device(query_gate, key_gate, value_seq, grad_output, filter_taps):
    parts = lax.axis_size("dp")
    blocks = lax.axis_size(BLOCK_AXES)
    devices = parts * blocks
    rows, channels = query_gate.shape
    per = channels // devices
    pieces = rows // LANES
    operands = (key_gate, value_seq, grad_output, query_gate, filter_taps)
    in_hbm = pl.BlockSpec(memory_space=pltpu.HBM)
    in_vmem = pl.BlockSpec(memory_space=pltpu.VMEM)
    gate = pltpu.VMEM((rows, channels), jnp.bfloat16)

    packed = pl.pallas_call(
        functools.partial(pack_kernel, parts, devices),
        out_shape=jax.ShapeDtypeStruct((channels * (2 * pieces + pieces // parts), LANES), jnp.float32),
        in_specs=[in_hbm] * 5,
        out_specs=in_vmem,
        scratch_shapes=[gate] * 4
        + [pltpu.VMEM((rows // parts, channels), jnp.float32), pltpu.SemaphoreType.DMA((5,))],
        compiler_params=params(32),
        name="pack",
    )(*(pltpu.with_memory_space_constraint(x, pltpu.HBM) for x in operands))
    received = exchange(packed, devices)
    results = pl.pallas_call(
        functools.partial(convolve_kernel, parts, blocks, per),
        out_shape=jax.ShapeDtypeStruct((3 * channels * pieces, LANES), jnp.float32),
        compiler_params=params(48),
        name="convolve",
    )(received, *tables(blocks, rows))
    returned = exchange(results, devices)
    narrow = jax.ShapeDtypeStruct((rows, channels), jnp.bfloat16)
    wide = jax.ShapeDtypeStruct((rows, channels), jnp.float32)
    return pl.pallas_call(
        functools.partial(unpack_kernel, devices, 1.0 / math.sqrt(blocks * rows)),
        out_shape=(narrow, narrow, narrow, wide),
        in_specs=[in_vmem] * 4,
        out_specs=[in_hbm] * 4,
        scratch_shapes=[gate] * 3
        + [pltpu.VMEM((rows, channels), jnp.float32), pltpu.SemaphoreType.DMA((4, pieces))],
        compiler_params=params(32),
        name="unpack",
    )(returned, key_gate, value_seq, grad_output)


def solution(mesh):
    split_rows = P(ALL_AXES, None)
    return jax.shard_map(
        per_device,
        mesh=mesh,
        in_specs=(split_rows, split_rows, split_rows, split_rows, P(BLOCK_AXES, None)),
        out_specs=(split_rows, split_rows, split_rows, split_rows),
        check_vma=False,
    )
```

```python
import functools
import math

import jax
import jax.numpy as jnp
import numpy as np
from jax import lax
from jax.experimental import pallas as pl
from jax.experimental.pallas import tpu as pltpu
from jax.sharding import PartitionSpec as P

BLOCK_AXES = ("outer", "inner")
ALL_AXES = ("dp",) + BLOCK_AXES
LANES = 128


def split_table(table):
    table = np.asarray(table, np.float32)
    high = table.astype(jnp.bfloat16)
    low = (table - high.astype(np.float32)).astype(jnp.bfloat16)
    return high, low


def tall_table(table):
    high, low = split_table(table)
    return np.concatenate([high, low, high], axis=0)


def tables(groups, width):
    pieces = width // LANES
    n1 = groups * pieces
    length = n1 * LANES
    group, low = np.arange(groups), np.arange(groups) + 0.25
    narrow, back = [], []
    for piece in range(pieces):
        turn = low[:, None] * (group[None, :] / groups + piece / n1) * (2.0 * math.pi)
        high_part, low_part = split_table(np.concatenate([np.cos(turn), -np.sin(turn)], axis=0))
        narrow.append(np.block([[high_part, high_part, low_part, low_part]]))
        high_part, low_part = split_table(np.concatenate([np.cos(turn.T), -np.sin(turn.T)], axis=1) / length)
        back.append(np.block([[high_part, high_part], [low_part, low_part]]))
    twist = (np.arange(n1) + 0.25)[:, None] * np.arange(LANES)[None, :] * (2.0 * math.pi / length)
    lane = np.arange(LANES)
    spin = lane[:, None] * lane[None, :] * (2.0 * math.pi / LANES)
    cos, sin = np.cos(spin), np.sin(spin)
    narrow += back + [tall_table(np.block([[cos, -sin], [sin, cos]])), tall_table(np.block([[cos, sin], [-sin, cos]]))]
    return np.concatenate(narrow, axis=0), np.stack([np.cos(twist), np.sin(twist)]).astype(np.float32)


def split(value):
    high = value.astype(jnp.bfloat16)
    low = (value - high.astype(jnp.float32)).astype(jnp.bfloat16)
    return high, low


def dot_wide(value, table):
    high, low = split(value)
    return jnp.dot(jnp.concatenate([high, high, low], axis=1), table, preferred_element_type=jnp.float32)


def pack_kernel(
    parts, devices, key_hbm, value_hbm, grad_hbm, query_hbm, taps_hbm, out_ref, key, value, grad, query, taps, sems
):
    rows, channels = key.shape
    pieces, per = rows // LANES, channels // devices
    taps_rows = rows // parts
    taps_pieces = taps_rows // LANES
    slab = per * (2 * pieces + taps_pieces)
    start = pl.multiple_of(lax.axis_index("dp") * taps_rows, taps_rows)

    def put(signal, first, count, piece):
        turned = signal.T
        for c in range(per):
            row = first + c * count + piece
            out_ref[pl.ds(row, devices, stride=slab), :] = turned[c * devices : (c + 1) * devices, :]

    def put_product(left, right, first):
        for piece in range(pieces):
            span = slice(piece * LANES, (piece + 1) * LANES)
            put(left[span, :].astype(jnp.float32) * right[span, :].astype(jnp.float32), first, pieces, piece)

    sources = (key_hbm, value_hbm, taps_hbm.at[pl.ds(start, taps_rows), :], grad_hbm, query_hbm)
    targets = (key, value, taps, grad, query)
    moves = [pltpu.make_async_copy(src, dst, sems.at[n]) for n, (src, dst) in enumerate(zip(sources, targets))]
    for move in moves:
        move.start()
    moves[0].wait()
    moves[1].wait()
    put_product(key, value, 0)
    moves[2].wait()
    for piece in range(taps_pieces):
        put(taps[piece * LANES : (piece + 1) * LANES, :], 2 * per * pieces, taps_pieces, piece)
    moves[3].wait()
    moves[4].wait()
    put_product(grad, query, per * pieces)


def unpack_kernel(
    devices, scale, in_ref, key_ref, value_ref, grad_ref, gq_hbm, gk_hbm, gv_hbm, gf_hbm, gq, gk, gv, gf, sems
):
    rows, channels = key_ref.shape
    pieces, per = rows // LANES, channels // devices
    slab = 3 * per * pieces

    def signal(s, piece):
        parts = [
            in_ref[pl.ds((s * per + c) * pieces + piece, devices, stride=slab), :] for c in range(per)
        ]
        return jnp.concatenate(parts, axis=0).T

    moves = []
    for piece in range(pieces):
        span = slice(piece * LANES, (piece + 1) * LANES)
        gq[span, :] = (grad_ref[span, :].astype(jnp.float32) * signal(0, piece)).astype(gq.dtype)
        corr = signal(1, piece)
        gk[span, :] = (corr * value_ref[span, :].astype(jnp.float32)).astype(gk.dtype)
        gv[span, :] = (corr * key_ref[span, :].astype(jnp.float32)).astype(gv.dtype)
        gf[span, :] = signal(2, piece) * scale
        for n, (src, dst) in enumerate(((gq, gq_hbm), (gk, gk_hbm), (gv, gv_hbm), (gf, gf_hbm))):
            here = pl.ds(piece * LANES, LANES)
            moves.append(pltpu.make_async_copy(src.at[here, :], dst.at[here, :], sems.at[n, piece]))
            moves[-1].start()
    for move in moves:
        move.wait()


def convolve_kernel(parts, blocks, per, in_ref, tables_ref, twist_ref, out_ref):
    n1 = twist_ref.shape[1]
    pieces = n1 // blocks
    taps_pieces = pieces // parts
    slab_in = per * (2 * pieces + taps_pieces)
    slab_out = 3 * per * pieces
    tall = 6 * LANES

    def table(start, rows):
        return tables_ref[start : start + rows, :]

    outer = [table(piece * LANES, LANES) for piece in range(pieces)]
    back_outer = [table((pieces + piece) * LANES, LANES) for piece in range(pieces)]
    inner, back_inner = (table(2 * pieces * LANES + n * tall, tall) for n in range(2))

    def load(row, part):
        return in_ref[pl.ds(part * blocks * slab_in + row, blocks, stride=slab_in), :]

    def load_signal(s, c, part):
        return [load((s * per + c) * pieces + piece, part) for piece in range(pieces)]

    def load_taps(c):
        first = 2 * pieces * per + c * taps_pieces
        return [load(first + piece % taps_pieces, piece // taps_pieces) for piece in range(pieces)]

    def butterfly(first, second, third, fourth, sign):
        sums = [a + b for a, b in zip(first, third)], [a + b for a, b in zip(second, fourth)]
        differences = [a - b for a, b in zip(first, third)], [a - b for a, b in zip(second, fourth)]
        (near_re, near_im), (far_re, far_im) = differences
        turned = [near_re - far_im, near_im + far_re], [near_re + far_im, near_im - far_re]
        return (
            [a + b for a, b in zip(*sums)],
            turned[0] if sign > 0 else turned[1],
            [a - b for a, b in zip(*sums)],
            turned[1] if sign > 0 else turned[0],
        )

    def outer_step(signals):
        parts_of = []
        for piece in range(pieces):
            high, low = split(jnp.concatenate([signal[piece] for signal in signals], axis=1))
            tall = jnp.concatenate([high, low, high, low], axis=0)
            sums = jnp.dot(outer[piece], tall, preferred_element_type=jnp.float32)
            parts_of.append((sums[:blocks], sums[blocks:]))
        spectra = butterfly(*parts_of, -1)
        turned = []
        for n in range(len(signals)):
            lanes = slice(n * LANES, (n + 1) * LANES)
            re, im = (jnp.concatenate([one[half][:, lanes] for one in spectra], axis=0) for half in range(2))
            cos, sin = twist_ref[0], twist_ref[1]
            turned.append(jnp.concatenate([re * cos + im * sin, im * cos - re * sin], axis=1))
        return jnp.concatenate(turned, axis=0)

    def inner_step(turned):
        done = dot_wide(turned, inner)
        return done[:, :LANES], done[:, LANES:]

    def product(left, right):
        return [left[0] * right[0] - left[1] * right[1], left[0] * right[1] + left[1] * right[0]]

    def product_conjugate(left, right):
        return [left[0] * right[0] + left[1] * right[1], left[1] * right[0] - left[0] * right[1]]

    def back_inner_step(products):
        done = dot_wide(jnp.concatenate(products, axis=1), back_inner)
        columns = []
        for n in range(parts):
            re, im = done[n * n1 : (n + 1) * n1, :LANES], done[n * n1 : (n + 1) * n1, LANES:]
            cos, sin = twist_ref[0], twist_ref[1]
            columns.append((re * cos - im * sin, re * sin + im * cos))
        return [jnp.concatenate(halves, axis=1) for halves in zip(*columns)]

    def back_outer_step(s, c, columns):
        quarters = ([half[n * blocks : (n + 1) * blocks] for half in columns] for n in range(pieces))
        for piece, turned in enumerate(butterfly(*quarters, 1)):
            tall = jnp.concatenate(split(jnp.concatenate(turned, axis=0)), axis=0)
            sums = jnp.dot(back_outer[piece], tall, preferred_element_type=jnp.float32)
            signals = sums[:blocks] + sums[blocks:]
            for part in range(parts):
                row = part * blocks * slab_out + (s * per + c) * pieces + piece
                out_ref[pl.ds(row, blocks, stride=slab_out), :] = signals[:, part * LANES : (part + 1) * LANES]

    def signal(s, c):
        return [load_signal(s, c, part) for part in range(parts)]

    def channel(pair, c):
        one = pair[c * n1 : (c + 1) * n1]
        return jnp.concatenate([one] * parts, axis=0)

    t = outer_step([load_taps(c) for c in range(per)])
    m0 = outer_step(signal(0, 0))
    g0 = outer_step(signal(1, 0))
    t = inner_step(t)
    taps = [[channel(half, c) for half in t] for c in range(per)]
    m0 = inner_step(m0)
    m1 = outer_step(signal(0, 1))
    g0 = inner_step(g0)
    conv0 = back_inner_step(product(m0, taps[0]))
    g1 = outer_step(signal(1, 1))
    corr0 = back_inner_step(product_conjugate(g0, taps[0]))
    back_outer_step(0, 0, conv0)
    cross0 = back_inner_step(product_conjugate(g0, m0))
    m1 = inner_step(m1)
    back_outer_step(1, 0, corr0)
    back_outer_step(2, 0, cross0)
    g1 = inner_step(g1)
    conv1 = back_inner_step(product(m1, taps[1]))
    corr1 = back_inner_step(product_conjugate(g1, taps[1]))
    cross1 = back_inner_step(product_conjugate(g1, m1))
    back_outer_step(0, 1, conv1)
    back_outer_step(1, 1, corr1)
    back_outer_step(2, 1, cross1)


def params(size):
    return pltpu.CompilerParams(vmem_limit_bytes=size << 20)


def exchange(slabs, devices):
    slabs = slabs.reshape(devices, -1, 4, LANES)
    slabs = lax.all_to_all(slabs, ALL_AXES, split_axis=0, concat_axis=0, tiled=True)
    return slabs.reshape(-1, LANES)


def per_device(query_gate, key_gate, value_seq, grad_output, filter_taps):
    parts = lax.axis_size("dp")
    blocks = lax.axis_size(BLOCK_AXES)
    devices = parts * blocks
    rows, channels = query_gate.shape
    per = channels // devices
    pieces = rows // LANES
    operands = (key_gate, value_seq, grad_output, query_gate, filter_taps)
    in_hbm = pl.BlockSpec(memory_space=pltpu.HBM)
    in_vmem = pl.BlockSpec(memory_space=pltpu.VMEM)
    gate = pltpu.VMEM((rows, channels), jnp.bfloat16)

    packed = pl.pallas_call(
        functools.partial(pack_kernel, parts, devices),
        out_shape=jax.ShapeDtypeStruct((channels * (2 * pieces + pieces // parts), LANES), jnp.float32),
        in_specs=[in_hbm] * 5,
        out_specs=in_vmem,
        scratch_shapes=[gate] * 4
        + [pltpu.VMEM((rows // parts, channels), jnp.float32), pltpu.SemaphoreType.DMA((5,))],
        compiler_params=params(32),
        name="pack",
    )(*(pltpu.with_memory_space_constraint(x, pltpu.HBM) for x in operands))
    received = exchange(packed, devices)
    results = pl.pallas_call(
        functools.partial(convolve_kernel, parts, blocks, per),
        out_shape=jax.ShapeDtypeStruct((3 * channels * pieces, LANES), jnp.float32),
        compiler_params=params(48),
        name="convolve",
    )(received, *tables(blocks, rows))
    returned = exchange(results, devices)
    narrow = jax.ShapeDtypeStruct((rows, channels), jnp.bfloat16)
    wide = jax.ShapeDtypeStruct((rows, channels), jnp.float32)
    return pl.pallas_call(
        functools.partial(unpack_kernel, devices, 1.0 / math.sqrt(blocks * rows)),
        out_shape=(narrow, narrow, narrow, wide),
        in_specs=[in_vmem] * 4,
        out_specs=[in_hbm] * 4,
        scratch_shapes=[gate] * 3
        + [pltpu.VMEM((rows, channels), jnp.float32), pltpu.SemaphoreType.DMA((4, pieces))],
        compiler_params=params(32),
        name="unpack",
    )(returned, key_gate, value_seq, grad_output)


def solution(mesh):
    split_rows = P(ALL_AXES, None)
    return jax.shard_map(
        per_device,
        mesh=mesh,
        in_specs=(split_rows, split_rows, split_rows, split_rows, P(BLOCK_AXES, None)),
        out_specs=(split_rows, split_rows, split_rows, split_rows),
        check_vma=False,
    )
```

```python
import functools
import math

import jax
import jax.numpy as jnp
import numpy as np
from jax import lax
from jax.experimental import pallas as pl
from jax.experimental.pallas import tpu as pltpu
from jax.sharding import PartitionSpec as P

BLOCK_AXES = ("outer", "inner")
ALL_AXES = ("dp",) + BLOCK_AXES
LANES = 128


def split_table(table):
    table = np.asarray(table, np.float32)
    high = table.astype(jnp.bfloat16)
    low = (table - high.astype(np.float32)).astype(jnp.bfloat16)
    return high, low


def tall_table(table):
    high, low = split_table(table)
    return np.concatenate([high, low, high], axis=0)


def tables(groups, width):
    pieces = width // LANES
    n1 = groups * pieces
    length = n1 * LANES
    group, low = np.arange(groups), np.arange(groups) + 0.25
    narrow, back = [], []
    for piece in range(pieces):
        turn = low[:, None] * (group[None, :] / groups + piece / n1) * (2.0 * math.pi)
        high_part, low_part = split_table(np.concatenate([np.cos(turn), -np.sin(turn)], axis=0))
        narrow.append(np.block([[high_part, high_part, low_part, low_part]]))
        high_part, low_part = split_table(np.concatenate([np.cos(turn.T), -np.sin(turn.T)], axis=1) / length)
        back.append(np.block([[high_part, high_part], [low_part, low_part]]))
    twist = (np.arange(n1) + 0.25)[:, None] * np.arange(LANES)[None, :] * (2.0 * math.pi / length)
    lane = np.arange(LANES)
    spin = lane[:, None] * lane[None, :] * (2.0 * math.pi / LANES)
    cos, sin = np.cos(spin), np.sin(spin)
    narrow += back + [tall_table(np.block([[cos, -sin], [sin, cos]]))]
    back_inner = np.block([[cos, sin], [-sin, cos]]).astype(np.float32)
    return np.concatenate(narrow, axis=0), back_inner, np.stack([np.cos(twist), np.sin(twist)]).astype(np.float32)


def split(value):
    high = value.astype(jnp.bfloat16)
    low = (value - high.astype(jnp.float32)).astype(jnp.bfloat16)
    return high, low


def dot_wide(value, table):
    high, low = split(value)
    return jnp.dot(jnp.concatenate([high, high, low], axis=1), table, preferred_element_type=jnp.float32)


def pack_kernel(
    parts, devices, key_hbm, value_hbm, grad_hbm, query_hbm, taps_hbm, out_ref, key, value, grad, query, taps, sems
):
    rows, channels = key.shape
    pieces, per = rows // LANES, channels // devices
    taps_rows = rows // parts
    taps_pieces = taps_rows // LANES
    slab = per * (2 * pieces + taps_pieces)
    start = pl.multiple_of(lax.axis_index("dp") * taps_rows, taps_rows)

    def put(signal, first, count, piece):
        turned = signal.T
        for c in range(per):
            row = first + c * count + piece
            out_ref[pl.ds(row, devices, stride=slab), :] = turned[c * devices : (c + 1) * devices, :]

    def put_product(left, right, first):
        for piece in range(pieces):
            span = slice(piece * LANES, (piece + 1) * LANES)
            put(left[span, :].astype(jnp.float32) * right[span, :].astype(jnp.float32), first, pieces, piece)

    sources = (key_hbm, value_hbm, taps_hbm.at[pl.ds(start, taps_rows), :], grad_hbm, query_hbm)
    targets = (key, value, taps, grad, query)
    moves = [pltpu.make_async_copy(src, dst, sems.at[n]) for n, (src, dst) in enumerate(zip(sources, targets))]
    for move in moves:
        move.start()
    moves[0].wait()
    moves[1].wait()
    put_product(key, value, 0)
    moves[2].wait()
    for piece in range(taps_pieces):
        put(taps[piece * LANES : (piece + 1) * LANES, :], 2 * per * pieces, taps_pieces, piece)
    moves[3].wait()
    moves[4].wait()
    put_product(grad, query, per * pieces)


def unpack_kernel(
    devices, scale, in_ref, key_ref, value_ref, grad_ref, gq_hbm, gk_hbm, gv_hbm, gf_hbm, gq, gk, gv, gf, sems
):
    rows, channels = key_ref.shape
    pieces, per = rows // LANES, channels // devices
    slab = 3 * per * pieces

    def signal(s, piece):
        parts = [
            in_ref[pl.ds((s * per + c) * pieces + piece, devices, stride=slab), :] for c in range(per)
        ]
        return jnp.concatenate(parts, axis=0).T

    moves = []
    for piece in range(pieces):
        span = slice(piece * LANES, (piece + 1) * LANES)
        gq[span, :] = (grad_ref[span, :].astype(jnp.float32) * signal(0, piece)).astype(gq.dtype)
        corr = signal(1, piece)
        gk[span, :] = (corr * value_ref[span, :].astype(jnp.float32)).astype(gk.dtype)
        gv[span, :] = (corr * key_ref[span, :].astype(jnp.float32)).astype(gv.dtype)
        gf[span, :] = signal(2, piece) * scale
        for n, (src, dst) in enumerate(((gq, gq_hbm), (gk, gk_hbm), (gv, gv_hbm), (gf, gf_hbm))):
            here = pl.ds(piece * LANES, LANES)
            moves.append(pltpu.make_async_copy(src.at[here, :], dst.at[here, :], sems.at[n, piece]))
            moves[-1].start()
    for move in moves:
        move.wait()


def convolve_kernel(parts, blocks, per, in_ref, tables_ref, back_inner_ref, twist_ref, out_ref):
    n1 = twist_ref.shape[1]
    pieces = n1 // blocks
    taps_pieces = pieces // parts
    slab_in = per * (2 * pieces + taps_pieces)
    slab_out = 3 * per * pieces

    def table(start, rows):
        return tables_ref[start : start + rows, :]

    outer = [table(piece * LANES, LANES) for piece in range(pieces)]
    back_outer = [table((pieces + piece) * LANES, LANES) for piece in range(pieces)]
    inner = table(2 * pieces * LANES, 6 * LANES)

    def load(row, part):
        return in_ref[pl.ds(part * blocks * slab_in + row, blocks, stride=slab_in), :]

    def load_signal(s, c, part):
        return [load((s * per + c) * pieces + piece, part) for piece in range(pieces)]

    def load_taps(c):
        first = 2 * pieces * per + c * taps_pieces
        return [load(first + piece % taps_pieces, piece // taps_pieces) for piece in range(pieces)]

    def butterfly(first, second, third, fourth, sign):
        sums = [a + b for a, b in zip(first, third)], [a + b for a, b in zip(second, fourth)]
        differences = [a - b for a, b in zip(first, third)], [a - b for a, b in zip(second, fourth)]
        (near_re, near_im), (far_re, far_im) = differences
        turned = [near_re - far_im, near_im + far_re], [near_re + far_im, near_im - far_re]
        return (
            [a + b for a, b in zip(*sums)],
            turned[0] if sign > 0 else turned[1],
            [a - b for a, b in zip(*sums)],
            turned[1] if sign > 0 else turned[0],
        )

    def outer_step(signals):
        parts_of = []
        for piece in range(pieces):
            high, low = split(jnp.concatenate([signal[piece] for signal in signals], axis=1))
            tall = jnp.concatenate([high, low, high, low], axis=0)
            sums = jnp.dot(outer[piece], tall, preferred_element_type=jnp.float32)
            parts_of.append((sums[:blocks], sums[blocks:]))
        spectra = butterfly(*parts_of, -1)
        turned = []
        for n in range(len(signals)):
            lanes = slice(n * LANES, (n + 1) * LANES)
            re, im = (jnp.concatenate([one[half][:, lanes] for one in spectra], axis=0) for half in range(2))
            cos, sin = twist_ref[0], twist_ref[1]
            turned.append(jnp.concatenate([re * cos + im * sin, im * cos - re * sin], axis=1))
        return jnp.concatenate(turned, axis=0)

    def inner_step(turned):
        done = dot_wide(turned, inner)
        return done[:, :LANES], done[:, LANES:]

    def product(left, right):
        return [left[0] * right[0] - left[1] * right[1], left[0] * right[1] + left[1] * right[0]]

    def product_conjugate(left, right):
        return [left[0] * right[0] + left[1] * right[1], left[1] * right[0] - left[0] * right[1]]

    def back_inner_step(products):
        done = jnp.dot(
            jnp.concatenate(products, axis=1),
            back_inner_ref[...],
            precision=lax.Precision.HIGH,
            preferred_element_type=jnp.float32,
        )
        columns = []
        for n in range(parts):
            re, im = done[n * n1 : (n + 1) * n1, :LANES], done[n * n1 : (n + 1) * n1, LANES:]
            cos, sin = twist_ref[0], twist_ref[1]
            columns.append((re * cos - im * sin, re * sin + im * cos))
        return [jnp.concatenate(halves, axis=1) for halves in zip(*columns)]

    def back_outer_step(s, c, columns):
        quarters = ([half[n * blocks : (n + 1) * blocks] for half in columns] for n in range(pieces))
        for piece, turned in enumerate(butterfly(*quarters, 1)):
            tall = jnp.concatenate(split(jnp.concatenate(turned, axis=0)), axis=0)
            sums = jnp.dot(back_outer[piece], tall, preferred_element_type=jnp.float32)
            signals = sums[:blocks] + sums[blocks:]
            for part in range(parts):
                row = part * blocks * slab_out + (s * per + c) * pieces + piece
                out_ref[pl.ds(row, blocks, stride=slab_out), :] = signals[:, part * LANES : (part + 1) * LANES]

    def signal(s, c):
        return [load_signal(s, c, part) for part in range(parts)]

    def channel(pair, c):
        one = pair[c * n1 : (c + 1) * n1]
        return jnp.concatenate([one] * parts, axis=0)

    t = outer_step([load_taps(c) for c in range(per)])
    m0 = outer_step(signal(0, 0))
    g0 = outer_step(signal(1, 0))
    t = inner_step(t)
    taps = [[channel(half, c) for half in t] for c in range(per)]
    m1 = outer_step(signal(0, 1))
    m0 = inner_step(m0)
    g0 = inner_step(g0)
    conv0 = back_inner_step(product(m0, taps[0]))
    g1 = outer_step(signal(1, 1))
    corr0 = back_inner_step(product_conjugate(g0, taps[0]))
    back_outer_step(0, 0, conv0)
    cross0 = back_inner_step(product_conjugate(g0, m0))
    m1 = inner_step(m1)
    back_outer_step(1, 0, corr0)
    g1 = inner_step(g1)
    back_outer_step(2, 0, cross0)
    conv1 = back_inner_step(product(m1, taps[1]))
    corr1 = back_inner_step(product_conjugate(g1, taps[1]))
    cross1 = back_inner_step(product_conjugate(g1, m1))
    back_outer_step(0, 1, conv1)
    back_outer_step(1, 1, corr1)
    back_outer_step(2, 1, cross1)


def params(size):
    return pltpu.CompilerParams(vmem_limit_bytes=size << 20)


def exchange(slabs, devices):
    slabs = slabs.reshape(devices, -1, 4, LANES)
    slabs = lax.all_to_all(slabs, ALL_AXES, split_axis=0, concat_axis=0, tiled=True)
    return slabs.reshape(-1, LANES)


def per_device(query_gate, key_gate, value_seq, grad_output, filter_taps):
    parts = lax.axis_size("dp")
    blocks = lax.axis_size(BLOCK_AXES)
    devices = parts * blocks
    rows, channels = query_gate.shape
    per = channels // devices
    pieces = rows // LANES
    operands = (key_gate, value_seq, grad_output, query_gate, filter_taps)
    in_hbm = pl.BlockSpec(memory_space=pltpu.HBM)
    in_vmem = pl.BlockSpec(memory_space=pltpu.VMEM)
    gate = pltpu.VMEM((rows, channels), jnp.bfloat16)

    packed = pl.pallas_call(
        functools.partial(pack_kernel, parts, devices),
        out_shape=jax.ShapeDtypeStruct((channels * (2 * pieces + pieces // parts), LANES), jnp.float32),
        in_specs=[in_hbm] * 5,
        out_specs=in_vmem,
        scratch_shapes=[gate] * 4
        + [pltpu.VMEM((rows // parts, channels), jnp.float32), pltpu.SemaphoreType.DMA((5,))],
        compiler_params=params(32),
        name="pack",
    )(*(pltpu.with_memory_space_constraint(x, pltpu.HBM) for x in operands))
    received = exchange(packed, devices)
    results = pl.pallas_call(
        functools.partial(convolve_kernel, parts, blocks, per),
        out_shape=jax.ShapeDtypeStruct((3 * channels * pieces, LANES), jnp.float32),
        compiler_params=params(48),
        name="convolve",
    )(received, *tables(blocks, rows))
    returned = exchange(results, devices)
    narrow = jax.ShapeDtypeStruct((rows, channels), jnp.bfloat16)
    wide = jax.ShapeDtypeStruct((rows, channels), jnp.float32)
    return pl.pallas_call(
        functools.partial(unpack_kernel, devices, 1.0 / math.sqrt(blocks * rows)),
        out_shape=(narrow, narrow, narrow, wide),
        in_specs=[in_vmem] * 4,
        out_specs=[in_hbm] * 4,
        scratch_shapes=[gate] * 3
        + [pltpu.VMEM((rows, channels), jnp.float32), pltpu.SemaphoreType.DMA((4, pieces))],
        compiler_params=params(32),
        name="unpack",
    )(returned, key_gate, value_seq, grad_output)


def solution(mesh):
    split_rows = P(ALL_AXES, None)
    return jax.shard_map(
        per_device,
        mesh=mesh,
        in_specs=(split_rows, split_rows, split_rows, split_rows, P(BLOCK_AXES, None)),
        out_specs=(split_rows, split_rows, split_rows, split_rows),
        check_vma=False,
    )
```

```python
import functools
import math

import jax
import jax.numpy as jnp
import numpy as np
from jax import lax
from jax.experimental import pallas as pl
from jax.experimental.pallas import tpu as pltpu
from jax.sharding import PartitionSpec as P

BLOCK_AXES = ("outer", "inner")
ALL_AXES = ("dp",) + BLOCK_AXES
LANES = 128


def split_table(table):
    table = np.asarray(table, np.float32)
    high = table.astype(jnp.bfloat16)
    low = (table - high.astype(np.float32)).astype(jnp.bfloat16)
    return high, low


def tall_table(table):
    high, low = split_table(table)
    return np.concatenate([high, low, high], axis=0)


def tables(groups, width):
    pieces = width // LANES
    n1 = groups * pieces
    length = n1 * LANES
    group, low = np.arange(groups), np.arange(groups) + 0.25
    narrow, back = [], []
    for piece in range(pieces):
        turn = low[:, None] * (group[None, :] / groups + piece / n1) * (2.0 * math.pi)
        high_part, low_part = split_table(np.concatenate([np.cos(turn), -np.sin(turn)], axis=0))
        narrow.append(np.block([[high_part, high_part, low_part, low_part]]))
        high_part, low_part = split_table(np.concatenate([np.cos(turn.T), -np.sin(turn.T)], axis=1) / length)
        back.append(np.block([[high_part, high_part], [low_part, low_part]]))
    twist = (np.arange(n1) + 0.25)[:, None] * np.arange(LANES)[None, :] * (2.0 * math.pi / length)
    lane = np.arange(LANES)
    spin = lane[:, None] * lane[None, :] * (2.0 * math.pi / LANES)
    cos, sin = np.cos(spin), np.sin(spin)
    narrow += back + [tall_table(np.block([[cos, -sin], [sin, cos]])), tall_table(np.block([[cos, sin], [-sin, cos]]))]
    return np.concatenate(narrow, axis=0), np.stack([np.cos(twist), np.sin(twist)]).astype(np.float32)


def split(value):
    high = value.astype(jnp.bfloat16)
    low = (value - high.astype(jnp.float32)).astype(jnp.bfloat16)
    return high, low


def dot_wide(value, table):
    high, low = split(value)
    return jnp.dot(jnp.concatenate([high, high, low], axis=1), table, preferred_element_type=jnp.float32)


def pack_kernel(
    parts, devices, key_hbm, value_hbm, grad_hbm, query_hbm, taps_hbm, out_ref, key, value, grad, query, taps, sems
):
    rows, channels = key.shape
    pieces, per = rows // LANES, channels // devices
    taps_rows = rows // parts
    taps_pieces = taps_rows // LANES
    slab = per * (2 * pieces + taps_pieces)
    start = pl.multiple_of(lax.axis_index("dp") * taps_rows, taps_rows)

    def put(signal, first, count, piece):
        turned = signal.T
        for c in range(per):
            row = first + c * count + piece
            out_ref[pl.ds(row, devices, stride=slab), :] = turned[c * devices : (c + 1) * devices, :]

    def put_product(left, right, first):
        for piece in range(pieces):
            span = slice(piece * LANES, (piece + 1) * LANES)
            put(left[span, :].astype(jnp.float32) * right[span, :].astype(jnp.float32), first, pieces, piece)

    sources = (taps_hbm.at[pl.ds(start, taps_rows), :], key_hbm, value_hbm, grad_hbm, query_hbm)
    targets = (taps, key, value, grad, query)
    moves = [pltpu.make_async_copy(src, dst, sems.at[n]) for n, (src, dst) in enumerate(zip(sources, targets))]
    for move in moves:
        move.start()
    moves[0].wait()
    for piece in range(taps_pieces):
        put(taps[piece * LANES : (piece + 1) * LANES, :], 2 * per * pieces, taps_pieces, piece)
    moves[1].wait()
    moves[2].wait()
    put_product(key, value, 0)
    moves[3].wait()
    moves[4].wait()
    put_product(grad, query, per * pieces)


def unpack_kernel(
    devices, scale, in_ref, key_ref, value_ref, grad_ref, gq_hbm, gk_hbm, gv_hbm, gf_hbm, gq, gk, gv, gf, sems
):
    rows, channels = key_ref.shape
    pieces, per = rows // LANES, channels // devices
    slab = 3 * per * pieces

    def signal(s, piece):
        parts = [
            in_ref[pl.ds((s * per + c) * pieces + piece, devices, stride=slab), :] for c in range(per)
        ]
        return jnp.concatenate(parts, axis=0).T

    moves = []
    for piece in range(pieces):
        span = slice(piece * LANES, (piece + 1) * LANES)
        gq[span, :] = (grad_ref[span, :].astype(jnp.float32) * signal(0, piece)).astype(gq.dtype)
        corr = signal(1, piece)
        gk[span, :] = (corr * value_ref[span, :].astype(jnp.float32)).astype(gk.dtype)
        gv[span, :] = (corr * key_ref[span, :].astype(jnp.float32)).astype(gv.dtype)
        gf[span, :] = signal(2, piece) * scale
        for n, (src, dst) in enumerate(((gq, gq_hbm), (gk, gk_hbm), (gv, gv_hbm), (gf, gf_hbm))):
            here = pl.ds(piece * LANES, LANES)
            moves.append(pltpu.make_async_copy(src.at[here, :], dst.at[here, :], sems.at[n, piece]))
            moves[-1].start()
    for move in moves:
        move.wait()


def convolve_kernel(parts, blocks, per, in_ref, tables_ref, twist_ref, out_ref):
    n1 = twist_ref.shape[1]
    pieces = n1 // blocks
    taps_pieces = pieces // parts
    slab_in = per * (2 * pieces + taps_pieces)
    slab_out = 3 * per * pieces
    tall = 6 * LANES

    def table(start, rows):
        return tables_ref[start : start + rows, :]

    outer = [table(piece * LANES, LANES) for piece in range(pieces)]
    back_outer = [table((pieces + piece) * LANES, LANES) for piece in range(pieces)]
    inner, back_inner = (table(2 * pieces * LANES + n * tall, tall) for n in range(2))

    def load(row, part):
        return in_ref[pl.ds(part * blocks * slab_in + row, blocks, stride=slab_in), :]

    def load_signal(s, c, part):
        return [load((s * per + c) * pieces + piece, part) for piece in range(pieces)]

    def load_taps(c):
        first = 2 * pieces * per + c * taps_pieces
        return [load(first + piece % taps_pieces, piece // taps_pieces) for piece in range(pieces)]

    def butterfly(first, second, third, fourth, sign):
        sums = [a + b for a, b in zip(first, third)], [a + b for a, b in zip(second, fourth)]
        differences = [a - b for a, b in zip(first, third)], [a - b for a, b in zip(second, fourth)]
        (near_re, near_im), (far_re, far_im) = differences
        turned = [near_re - far_im, near_im + far_re], [near_re + far_im, near_im - far_re]
        return (
            [a + b for a, b in zip(*sums)],
            turned[0] if sign > 0 else turned[1],
            [a - b for a, b in zip(*sums)],
            turned[1] if sign > 0 else turned[0],
        )

    def outer_step(signals):
        parts_of = []
        for piece in range(pieces):
            high, low = split(jnp.concatenate([signal[piece] for signal in signals], axis=1))
            tall = jnp.concatenate([high, low, high, low], axis=0)
            sums = jnp.dot(outer[piece], tall, preferred_element_type=jnp.float32)
            parts_of.append((sums[:blocks], sums[blocks:]))
        spectra = butterfly(*parts_of, -1)
        turned = []
        for n in range(len(signals)):
            lanes = slice(n * LANES, (n + 1) * LANES)
            re, im = (jnp.concatenate([one[half][:, lanes] for one in spectra], axis=0) for half in range(2))
            cos, sin = twist_ref[0], twist_ref[1]
            turned.append(jnp.concatenate([re * cos + im * sin, im * cos - re * sin], axis=1))
        return jnp.concatenate(turned, axis=0)

    def inner_step(turned):
        done = dot_wide(turned, inner)
        return done[:, :LANES], done[:, LANES:]

    def product(left, right):
        return [left[0] * right[0] - left[1] * right[1], left[0] * right[1] + left[1] * right[0]]

    def product_conjugate(left, right):
        return [left[0] * right[0] + left[1] * right[1], left[1] * right[0] - left[0] * right[1]]

    def back_inner_step(products):
        done = dot_wide(jnp.concatenate(products, axis=1), back_inner)
        columns = []
        for n in range(parts):
            re, im = done[n * n1 : (n + 1) * n1, :LANES], done[n * n1 : (n + 1) * n1, LANES:]
            cos, sin = twist_ref[0], twist_ref[1]
            columns.append((re * cos - im * sin, re * sin + im * cos))
        return [jnp.concatenate(halves, axis=1) for halves in zip(*columns)]

    def back_outer_step(s, c, columns):
        quarters = ([half[n * blocks : (n + 1) * blocks] for half in columns] for n in range(pieces))
        for piece, turned in enumerate(butterfly(*quarters, 1)):
            tall = jnp.concatenate(split(jnp.concatenate(turned, axis=0)), axis=0)
            sums = jnp.dot(back_outer[piece], tall, preferred_element_type=jnp.float32)
            signals = sums[:blocks] + sums[blocks:]
            for part in range(parts):
                row = part * blocks * slab_out + (s * per + c) * pieces + piece
                out_ref[pl.ds(row, blocks, stride=slab_out), :] = signals[:, part * LANES : (part + 1) * LANES]

    def signal(s, c):
        return [load_signal(s, c, part) for part in range(parts)]

    def channel(pair, c):
        one = pair[c * n1 : (c + 1) * n1]
        return jnp.concatenate([one] * parts, axis=0)

    t = outer_step([load_taps(c) for c in range(per)])
    m0 = outer_step(signal(0, 0))
    g0 = outer_step(signal(1, 0))
    t = inner_step(t)
    taps = [[channel(half, c) for half in t] for c in range(per)]
    m0 = inner_step(m0)
    m1 = outer_step(signal(0, 1))
    g0 = inner_step(g0)
    conv0 = back_inner_step(product(m0, taps[0]))
    g1 = outer_step(signal(1, 1))
    corr0 = back_inner_step(product_conjugate(g0, taps[0]))
    back_outer_step(0, 0, conv0)
    cross0 = back_inner_step(product_conjugate(g0, m0))
    m1 = inner_step(m1)
    back_outer_step(1, 0, corr0)
    back_outer_step(2, 0, cross0)
    g1 = inner_step(g1)
    conv1 = back_inner_step(product(m1, taps[1]))
    corr1 = back_inner_step(product_conjugate(g1, taps[1]))
    cross1 = back_inner_step(product_conjugate(g1, m1))
    back_outer_step(0, 1, conv1)
    back_outer_step(1, 1, corr1)
    back_outer_step(2, 1, cross1)


def params(size):
    return pltpu.CompilerParams(vmem_limit_bytes=size << 20)


def exchange(slabs, devices):
    slabs = slabs.reshape(devices, -1, 4, LANES)
    slabs = lax.all_to_all(slabs, ALL_AXES, split_axis=0, concat_axis=0, tiled=True)
    return slabs.reshape(-1, LANES)


def per_device(query_gate, key_gate, value_seq, grad_output, filter_taps):
    parts = lax.axis_size("dp")
    blocks = lax.axis_size(BLOCK_AXES)
    devices = parts * blocks
    rows, channels = query_gate.shape
    per = channels // devices
    pieces = rows // LANES
    operands = (key_gate, value_seq, grad_output, query_gate, filter_taps)
    in_hbm = pl.BlockSpec(memory_space=pltpu.HBM)
    in_vmem = pl.BlockSpec(memory_space=pltpu.VMEM)
    gate = pltpu.VMEM((rows, channels), jnp.bfloat16)

    packed = pl.pallas_call(
        functools.partial(pack_kernel, parts, devices),
        out_shape=jax.ShapeDtypeStruct((channels * (2 * pieces + pieces // parts), LANES), jnp.float32),
        in_specs=[in_hbm] * 5,
        out_specs=in_vmem,
        scratch_shapes=[gate] * 4
        + [pltpu.VMEM((rows // parts, channels), jnp.float32), pltpu.SemaphoreType.DMA((5,))],
        compiler_params=params(32),
        name="pack",
    )(*(pltpu.with_memory_space_constraint(x, pltpu.HBM) for x in operands))
    received = exchange(packed, devices)
    results = pl.pallas_call(
        functools.partial(convolve_kernel, parts, blocks, per),
        out_shape=jax.ShapeDtypeStruct((3 * channels * pieces, LANES), jnp.float32),
        compiler_params=params(48),
        name="convolve",
    )(received, *tables(blocks, rows))
    returned = exchange(results, devices)
    narrow = jax.ShapeDtypeStruct((rows, channels), jnp.bfloat16)
    wide = jax.ShapeDtypeStruct((rows, channels), jnp.float32)
    return pl.pallas_call(
        functools.partial(unpack_kernel, devices, 1.0 / math.sqrt(blocks * rows)),
        out_shape=(narrow, narrow, narrow, wide),
        in_specs=[in_vmem] * 4,
        out_specs=[in_hbm] * 4,
        scratch_shapes=[gate] * 3
        + [pltpu.VMEM((rows, channels), jnp.float32), pltpu.SemaphoreType.DMA((4, pieces))],
        compiler_params=params(32),
        name="unpack",
    )(returned, key_gate, value_seq, grad_output)


def solution(mesh):
    split_rows = P(ALL_AXES, None)
    return jax.shard_map(
        per_device,
        mesh=mesh,
        in_specs=(split_rows, split_rows, split_rows, split_rows, P(BLOCK_AXES, None)),
        out_specs=(split_rows, split_rows, split_rows, split_rows),
        check_vma=False,
    )
```

```python
import functools
import math

import jax
import jax.numpy as jnp
import numpy as np
from jax import lax
from jax.experimental import pallas as pl
from jax.experimental.pallas import tpu as pltpu
from jax.sharding import PartitionSpec as P

BLOCK_AXES = ("outer", "inner")
ALL_AXES = ("dp",) + BLOCK_AXES
LANES = 128


def split_table(table):
    table = np.asarray(table, np.float32)
    high = table.astype(jnp.bfloat16)
    low = (table - high.astype(np.float32)).astype(jnp.bfloat16)
    return high, low


def tall_table(table):
    high, low = split_table(table)
    return np.concatenate([high, low, high], axis=0)


def tables(groups, width):
    pieces = width // LANES
    n1 = groups * pieces
    length = n1 * LANES
    group, low = np.arange(groups), np.arange(groups) + 0.25
    narrow, back = [], []
    for piece in range(pieces):
        turn = low[:, None] * (group[None, :] / groups + piece / n1) * (2.0 * math.pi)
        high_part, low_part = split_table(np.concatenate([np.cos(turn), -np.sin(turn)], axis=0))
        narrow.append(np.block([[high_part, high_part, low_part, low_part]]))
        high_part, low_part = split_table(np.concatenate([np.cos(turn.T), -np.sin(turn.T)], axis=1) / length)
        back.append(np.block([[high_part, high_part], [low_part, low_part]]))
    twist = (np.arange(n1) + 0.25)[:, None] * np.arange(LANES)[None, :] * (2.0 * math.pi / length)
    lane = np.arange(LANES)
    spin = lane[:, None] * lane[None, :] * (2.0 * math.pi / LANES)
    cos, sin = np.cos(spin), np.sin(spin)
    narrow += back + [tall_table(np.block([[cos, -sin], [sin, cos]])), tall_table(np.block([[cos, sin], [-sin, cos]]))]
    return np.concatenate(narrow, axis=0), np.stack([np.cos(twist), np.sin(twist)]).astype(np.float32)


def split(value):
    high = value.astype(jnp.bfloat16)
    low = (value - high.astype(jnp.float32)).astype(jnp.bfloat16)
    return high, low


def dot_wide(value, table):
    high, low = value
    return jnp.dot(jnp.concatenate([high, high, low], axis=1), table, preferred_element_type=jnp.float32)


def pack_kernel(
    parts, devices, key_hbm, value_hbm, grad_hbm, query_hbm, taps_hbm, out_ref, key, value, grad, query, taps, sems
):
    rows, channels = key.shape
    pieces, per = rows // LANES, channels // devices
    taps_rows = rows // parts
    taps_pieces = taps_rows // LANES
    slab = per * (2 * pieces + taps_pieces)
    start = pl.multiple_of(lax.axis_index("dp") * taps_rows, taps_rows)

    def put(signal, first, count, piece):
        turned = signal.T
        for c in range(per):
            row = first + c * count + piece
            out_ref[pl.ds(row, devices, stride=slab), :] = turned[c * devices : (c + 1) * devices, :]

    def put_product(left, right, first):
        for piece in range(pieces):
            span = slice(piece * LANES, (piece + 1) * LANES)
            put(left[span, :].astype(jnp.float32) * right[span, :].astype(jnp.float32), first, pieces, piece)

    sources = (key_hbm, value_hbm, taps_hbm.at[pl.ds(start, taps_rows), :], grad_hbm, query_hbm)
    targets = (key, value, taps, grad, query)
    moves = [pltpu.make_async_copy(src, dst, sems.at[n]) for n, (src, dst) in enumerate(zip(sources, targets))]
    for move in moves:
        move.start()
    moves[0].wait()
    moves[1].wait()
    put_product(key, value, 0)
    moves[2].wait()
    for piece in range(taps_pieces):
        put(taps[piece * LANES : (piece + 1) * LANES, :], 2 * per * pieces, taps_pieces, piece)
    moves[3].wait()
    moves[4].wait()
    put_product(grad, query, per * pieces)


def unpack_kernel(
    devices, scale, in_ref, key_ref, value_ref, grad_ref, gq_hbm, gk_hbm, gv_hbm, gf_hbm, gq, gk, gv, gf, sems
):
    rows, channels = key_ref.shape
    pieces, per = rows // LANES, channels // devices
    slab = 3 * per * pieces

    def signal(s, piece):
        parts = [
            in_ref[pl.ds((s * per + c) * pieces + piece, devices, stride=slab), :] for c in range(per)
        ]
        return jnp.concatenate(parts, axis=0).T

    moves = []
    for piece in range(pieces):
        span = slice(piece * LANES, (piece + 1) * LANES)
        gq[span, :] = (grad_ref[span, :].astype(jnp.float32) * signal(0, piece)).astype(gq.dtype)
        corr = signal(1, piece)
        gk[span, :] = (corr * value_ref[span, :].astype(jnp.float32)).astype(gk.dtype)
        gv[span, :] = (corr * key_ref[span, :].astype(jnp.float32)).astype(gv.dtype)
        gf[span, :] = signal(2, piece) * scale
        for n, (src, dst) in enumerate(((gq, gq_hbm), (gk, gk_hbm), (gv, gv_hbm), (gf, gf_hbm))):
            here = pl.ds(piece * LANES, LANES)
            moves.append(pltpu.make_async_copy(src.at[here, :], dst.at[here, :], sems.at[n, piece]))
            moves[-1].start()
    for move in moves:
        move.wait()


def convolve_kernel(parts, blocks, per, in_ref, tables_ref, twist_ref, out_ref):
    n1 = twist_ref.shape[1]
    pieces = n1 // blocks
    taps_pieces = pieces // parts
    slab_in = per * (2 * pieces + taps_pieces)
    slab_out = 3 * per * pieces
    tall = 6 * LANES

    def table(start, rows):
        return tables_ref[start : start + rows, :]

    outer = [table(piece * LANES, LANES) for piece in range(pieces)]
    back_outer = [table((pieces + piece) * LANES, LANES) for piece in range(pieces)]
    inner, back_inner = (table(2 * pieces * LANES + n * tall, tall) for n in range(2))

    def load(row, part):
        return in_ref[pl.ds(part * blocks * slab_in + row, blocks, stride=slab_in), :]

    def load_signal(s, c, part):
        return [load((s * per + c) * pieces + piece, part) for piece in range(pieces)]

    def load_taps(c):
        first = 2 * pieces * per + c * taps_pieces
        return [load(first + piece % taps_pieces, piece // taps_pieces) for piece in range(pieces)]

    def butterfly(first, second, third, fourth, sign):
        sums = [a + b for a, b in zip(first, third)], [a + b for a, b in zip(second, fourth)]
        differences = [a - b for a, b in zip(first, third)], [a - b for a, b in zip(second, fourth)]
        (near_re, near_im), (far_re, far_im) = differences
        turned = [near_re - far_im, near_im + far_re], [near_re + far_im, near_im - far_re]
        return (
            [a + b for a, b in zip(*sums)],
            turned[0] if sign > 0 else turned[1],
            [a - b for a, b in zip(*sums)],
            turned[1] if sign > 0 else turned[0],
        )

    def outer_products(signals):
        parts_of = []
        for piece in range(pieces):
            high, low = split(jnp.concatenate([signal[piece] for signal in signals], axis=1))
            tall = jnp.concatenate([high, low, high, low], axis=0)
            sums = jnp.dot(outer[piece], tall, preferred_element_type=jnp.float32)
            parts_of.append((sums[:blocks], sums[blocks:]))
        return parts_of

    def outer_turns(parts_of):
        spectra = butterfly(*parts_of, -1)
        turned = []
        for n in range(parts):
            lanes = slice(n * LANES, (n + 1) * LANES)
            re, im = (jnp.concatenate([one[half][:, lanes] for one in spectra], axis=0) for half in range(2))
            cos, sin = twist_ref[0], twist_ref[1]
            turned.append(jnp.concatenate([re * cos + im * sin, im * cos - re * sin], axis=1))
        return split(jnp.concatenate(turned, axis=0))

    def inner_products(turned):
        done = dot_wide(turned, inner)
        return done[:, :LANES], done[:, LANES:]

    def product(left, right):
        re, im = left[0] * right[0] - left[1] * right[1], left[0] * right[1] + left[1] * right[0]
        return split(jnp.concatenate([re, im], axis=1))

    def product_conjugate(left, right):
        re, im = left[0] * right[0] + left[1] * right[1], left[1] * right[0] - left[0] * right[1]
        return split(jnp.concatenate([re, im], axis=1))

    def back_turns(done):
        columns = []
        for n in range(parts):
            re, im = done[n * n1 : (n + 1) * n1, :LANES], done[n * n1 : (n + 1) * n1, LANES:]
            cos, sin = twist_ref[0], twist_ref[1]
            columns.append((re * cos - im * sin, re * sin + im * cos))
        halves = [jnp.concatenate(half, axis=1) for half in zip(*columns)]
        quarters = ([half[n * blocks : (n + 1) * blocks] for half in halves] for n in range(pieces))
        turns = butterfly(*quarters, 1)
        return [jnp.concatenate(split(jnp.concatenate(turned, axis=0)), axis=0) for turned in turns]

    def back_outer_products(s, c, talls):
        for piece, tall in enumerate(talls):
            sums = jnp.dot(back_outer[piece], tall, preferred_element_type=jnp.float32)
            signals = sums[:blocks] + sums[blocks:]
            for part in range(parts):
                row = part * blocks * slab_out + (s * per + c) * pieces + piece
                out_ref[pl.ds(row, blocks, stride=slab_out), :] = signals[:, part * LANES : (part + 1) * LANES]

    def signal(s, c):
        return [load_signal(s, c, part) for part in range(parts)]

    def channel(pair, c):
        one = pair[c * n1 : (c + 1) * n1]
        return jnp.concatenate([one] * parts, axis=0)

    grad1 = outer_products(signal(1, 1))
    mixed0 = outer_products(signal(0, 0))
    grad1 = outer_turns(grad1)
    grad0 = outer_products(signal(1, 0))
    mixed0 = outer_turns(mixed0)
    taps = outer_products([load_taps(c) for c in range(per)])
    grad0 = outer_turns(grad0)
    mixed1 = outer_products(signal(0, 1))
    grad1 = inner_products(grad1)
    taps = outer_turns(taps)
    taps = inner_products(taps)
    taps = [[channel(half, c) for half in taps] for c in range(per)]
    corr1 = product_conjugate(grad1, taps[1])
    mixed1 = outer_turns(mixed1)
    mixed1 = inner_products(mixed1)
    grad0 = inner_products(grad0)
    conv1 = product(mixed1, taps[1])
    cross1 = product_conjugate(grad1, mixed1)
    mixed0 = inner_products(mixed0)
    cross0 = product_conjugate(grad0, mixed0)
    corr0 = product_conjugate(grad0, taps[0])
    corr0 = dot_wide(corr0, back_inner)
    cross0 = dot_wide(cross0, back_inner)
    conv0 = product(mixed0, taps[0])
    corr0 = back_turns(corr0)
    corr1 = dot_wide(corr1, back_inner)
    cross0 = back_turns(cross0)
    conv1 = dot_wide(conv1, back_inner)
    corr1 = back_turns(corr1)
    back_outer_products(1, 0, corr0)
    conv1 = back_turns(conv1)
    conv0 = dot_wide(conv0, back_inner)
    conv0 = back_turns(conv0)
    cross1 = dot_wide(cross1, back_inner)
    back_outer_products(0, 0, conv0)
    cross1 = back_turns(cross1)
    back_outer_products(2, 0, cross0)
    back_outer_products(2, 1, cross1)
    back_outer_products(0, 1, conv1)
    back_outer_products(1, 1, corr1)


def params(size):
    return pltpu.CompilerParams(vmem_limit_bytes=size << 20)


def exchange(slabs, devices):
    slabs = slabs.reshape(devices, -1, 4, LANES)
    slabs = lax.all_to_all(slabs, ALL_AXES, split_axis=0, concat_axis=0, tiled=True)
    return slabs.reshape(-1, LANES)


def per_device(query_gate, key_gate, value_seq, grad_output, filter_taps):
    parts = lax.axis_size("dp")
    blocks = lax.axis_size(BLOCK_AXES)
    devices = parts * blocks
    rows, channels = query_gate.shape
    per = channels // devices
    pieces = rows // LANES
    operands = (key_gate, value_seq, grad_output, query_gate, filter_taps)
    in_hbm = pl.BlockSpec(memory_space=pltpu.HBM)
    in_vmem = pl.BlockSpec(memory_space=pltpu.VMEM)
    gate = pltpu.VMEM((rows, channels), jnp.bfloat16)

    packed = pl.pallas_call(
        functools.partial(pack_kernel, parts, devices),
        out_shape=jax.ShapeDtypeStruct((channels * (2 * pieces + pieces // parts), LANES), jnp.float32),
        in_specs=[in_hbm] * 5,
        out_specs=in_vmem,
        scratch_shapes=[gate] * 4
        + [pltpu.VMEM((rows // parts, channels), jnp.float32), pltpu.SemaphoreType.DMA((5,))],
        compiler_params=params(32),
        name="pack",
    )(*(pltpu.with_memory_space_constraint(x, pltpu.HBM) for x in operands))
    received = exchange(packed, devices)
    results = pl.pallas_call(
        functools.partial(convolve_kernel, parts, blocks, per),
        out_shape=jax.ShapeDtypeStruct((3 * channels * pieces, LANES), jnp.float32),
        compiler_params=params(48),
        name="convolve",
    )(received, *tables(blocks, rows))
    returned = exchange(results, devices)
    narrow = jax.ShapeDtypeStruct((rows, channels), jnp.bfloat16)
    wide = jax.ShapeDtypeStruct((rows, channels), jnp.float32)
    return pl.pallas_call(
        functools.partial(unpack_kernel, devices, 1.0 / math.sqrt(blocks * rows)),
        out_shape=(narrow, narrow, narrow, wide),
        in_specs=[in_vmem] * 4,
        out_specs=[in_hbm] * 4,
        scratch_shapes=[gate] * 3
        + [pltpu.VMEM((rows, channels), jnp.float32), pltpu.SemaphoreType.DMA((4, pieces))],
        compiler_params=params(32),
        name="unpack",
    )(returned, key_gate, value_seq, grad_output)


def solution(mesh):
    split_rows = P(ALL_AXES, None)
    return jax.shard_map(
        per_device,
        mesh=mesh,
        in_specs=(split_rows, split_rows, split_rows, split_rows, P(BLOCK_AXES, None)),
        out_specs=(split_rows, split_rows, split_rows, split_rows),
        check_vma=False,
    )
```

```python
import functools
import math

import jax
import jax.numpy as jnp
import numpy as np
from jax import lax
from jax.experimental import pallas as pl
from jax.experimental.pallas import tpu as pltpu
from jax.sharding import PartitionSpec as P

BLOCK_AXES = ("outer", "inner")
ALL_AXES = ("dp",) + BLOCK_AXES
LANES = 128


def split_table(table):
    table = np.asarray(table, np.float32)
    high = table.astype(jnp.bfloat16)
    low = (table - high.astype(np.float32)).astype(jnp.bfloat16)
    return high, low


def tall_table(table):
    high, low = split_table(table)
    return np.concatenate([high, low, high], axis=0)


def tables(groups, width):
    pieces = width // LANES
    n1 = groups * pieces
    length = n1 * LANES
    group, low = np.arange(groups), np.arange(groups) + 0.25
    narrow, back = [], []
    for piece in range(pieces):
        turn = low[:, None] * (group[None, :] / groups + piece / n1) * (2.0 * math.pi)
        high_part, low_part = split_table(np.concatenate([np.cos(turn), -np.sin(turn)], axis=0))
        narrow.append(np.block([[high_part, high_part, low_part, low_part]]))
        high_part, low_part = split_table(np.concatenate([np.cos(turn.T), -np.sin(turn.T)], axis=1) / length)
        back.append(np.block([[high_part, high_part], [low_part, low_part]]))
    twist = (np.arange(n1) + 0.25)[:, None] * np.arange(LANES)[None, :] * (2.0 * math.pi / length)
    lane = np.arange(LANES)
    spin = lane[:, None] * lane[None, :] * (2.0 * math.pi / LANES)
    cos, sin = np.cos(spin), np.sin(spin)
    narrow += back + [tall_table(np.block([[cos, -sin], [sin, cos]])), tall_table(np.block([[cos, sin], [-sin, cos]]))]
    return np.concatenate(narrow, axis=0), np.stack([np.cos(twist), np.sin(twist)]).astype(np.float32)


def split(value):
    high = value.astype(jnp.bfloat16)
    low = (value - high.astype(jnp.float32)).astype(jnp.bfloat16)
    return high, low


def dot_wide(value, table):
    high, low = split(value)
    return jnp.dot(jnp.concatenate([high, high, low], axis=1), table, preferred_element_type=jnp.float32)


def pack_kernel(
    parts, devices, key_hbm, value_hbm, grad_hbm, query_hbm, taps_hbm, out_ref, key, value, grad, query, taps, sems
):
    rows, channels = key.shape
    pieces, per = rows // LANES, channels // devices
    taps_rows = rows // parts
    taps_pieces = taps_rows // LANES
    slab = per * (2 * pieces + taps_pieces)
    start = pl.multiple_of(lax.axis_index("dp") * taps_rows, taps_rows)

    def put(signal, first, count, piece):
        turned = signal.T
        for c in range(per):
            row = first + c * count + piece
            out_ref[pl.ds(row, devices, stride=slab), :] = turned[c * devices : (c + 1) * devices, :]

    def put_product(left, right, first):
        for piece in range(pieces):
            span = slice(piece * LANES, (piece + 1) * LANES)
            put(left[span, :].astype(jnp.float32) * right[span, :].astype(jnp.float32), first, pieces, piece)

    sources = (key_hbm, value_hbm, taps_hbm.at[pl.ds(start, taps_rows), :], grad_hbm, query_hbm)
    targets = (key, value, taps, grad, query)
    moves = [pltpu.make_async_copy(src, dst, sems.at[n]) for n, (src, dst) in enumerate(zip(sources, targets))]
    for move in moves:
        move.start()
    moves[0].wait()
    moves[1].wait()
    put_product(key, value, 0)
    moves[2].wait()
    for piece in range(taps_pieces):
        put(taps[piece * LANES : (piece + 1) * LANES, :], 2 * per * pieces, taps_pieces, piece)
    moves[3].wait()
    moves[4].wait()
    put_product(grad, query, per * pieces)


def unpack_kernel(
    devices, scale, in_ref, key_ref, value_ref, grad_ref, gq_hbm, gk_hbm, gv_hbm, gf_hbm, gq, gk, gv, gf, sems
):
    rows, channels = key_ref.shape
    pieces, per = rows // LANES, channels // devices
    slab = 3 * per * pieces

    def signal(s, piece):
        parts = [
            in_ref[pl.ds((s * per + c) * pieces + piece, devices, stride=slab), :] for c in range(per)
        ]
        return jnp.concatenate(parts, axis=0).T

    moves = []
    for piece in range(pieces):
        span = slice(piece * LANES, (piece + 1) * LANES)
        here = pl.ds(piece * LANES, LANES)

        def send(n, src, dst):
            moves.append(pltpu.make_async_copy(src.at[here, :], dst.at[here, :], sems.at[n, piece]))
            moves[-1].start()

        gf[span, :] = signal(2, piece) * scale
        send(3, gf, gf_hbm)
        corr = signal(1, piece)
        gk[span, :] = (corr * value_ref[span, :].astype(jnp.float32)).astype(gk.dtype)
        send(1, gk, gk_hbm)
        gv[span, :] = (corr * key_ref[span, :].astype(jnp.float32)).astype(gv.dtype)
        send(2, gv, gv_hbm)
        gq[span, :] = (grad_ref[span, :].astype(jnp.float32) * signal(0, piece)).astype(gq.dtype)
        send(0, gq, gq_hbm)
    for move in moves:
        move.wait()


def convolve_kernel(parts, blocks, per, in_ref, tables_ref, twist_ref, out_ref):
    n1 = twist_ref.shape[1]
    pieces = n1 // blocks
    taps_pieces = pieces // parts
    slab_in = per * (2 * pieces + taps_pieces)
    slab_out = 3 * per * pieces
    tall = 6 * LANES

    def table(start, rows):
        return tables_ref[start : start + rows, :]

    outer = [table(piece * LANES, LANES) for piece in range(pieces)]
    back_outer = [table((pieces + piece) * LANES, LANES) for piece in range(pieces)]
    inner, back_inner = (table(2 * pieces * LANES + n * tall, tall) for n in range(2))

    def load(row, part):
        return in_ref[pl.ds(part * blocks * slab_in + row, blocks, stride=slab_in), :]

    def load_signal(s, c, part):
        return [load((s * per + c) * pieces + piece, part) for piece in range(pieces)]

    def load_taps(c):
        first = 2 * pieces * per + c * taps_pieces
        return [load(first + piece % taps_pieces, piece // taps_pieces) for piece in range(pieces)]

    def butterfly(first, second, third, fourth, sign):
        sums = [a + b for a, b in zip(first, third)], [a + b for a, b in zip(second, fourth)]
        differences = [a - b for a, b in zip(first, third)], [a - b for a, b in zip(second, fourth)]
        (near_re, near_im), (far_re, far_im) = differences
        turned = [near_re - far_im, near_im + far_re], [near_re + far_im, near_im - far_re]
        return (
            [a + b for a, b in zip(*sums)],
            turned[0] if sign > 0 else turned[1],
            [a - b for a, b in zip(*sums)],
            turned[1] if sign > 0 else turned[0],
        )

    def outer_step(signals):
        parts_of = []
        for piece in range(pieces):
            high, low = split(jnp.concatenate([signal[piece] for signal in signals], axis=1))
            tall = jnp.concatenate([high, low, high, low], axis=0)
            sums = jnp.dot(outer[piece], tall, preferred_element_type=jnp.float32)
            parts_of.append((sums[:blocks], sums[blocks:]))
        spectra = butterfly(*parts_of, -1)
        turned = []
        for n in range(len(signals)):
            lanes = slice(n * LANES, (n + 1) * LANES)
            re, im = (jnp.concatenate([one[half][:, lanes] for one in spectra], axis=0) for half in range(2))
            cos, sin = twist_ref[0], twist_ref[1]
            turned.append(jnp.concatenate([re * cos + im * sin, im * cos - re * sin], axis=1))
        return jnp.concatenate(turned, axis=0)

    def inner_step(turned):
        done = dot_wide(turned, inner)
        return done[:, :LANES], done[:, LANES:]

    def product(left, right):
        return [left[0] * right[0] - left[1] * right[1], left[0] * right[1] + left[1] * right[0]]

    def product_conjugate(left, right):
        return [left[0] * right[0] + left[1] * right[1], left[1] * right[0] - left[0] * right[1]]

    def back_inner_step(products):
        done = dot_wide(jnp.concatenate(products, axis=1), back_inner)
        columns = []
        for n in range(parts):
            re, im = done[n * n1 : (n + 1) * n1, :LANES], done[n * n1 : (n + 1) * n1, LANES:]
            cos, sin = twist_ref[0], twist_ref[1]
            columns.append((re * cos - im * sin, re * sin + im * cos))
        return [jnp.concatenate(halves, axis=1) for halves in zip(*columns)]

    def back_outer_step(s, c, columns):
        quarters = ([half[n * blocks : (n + 1) * blocks] for half in columns] for n in range(pieces))
        for piece, turned in enumerate(butterfly(*quarters, 1)):
            tall = jnp.concatenate(split(jnp.concatenate(turned, axis=0)), axis=0)
            sums = jnp.dot(back_outer[piece], tall, preferred_element_type=jnp.float32)
            signals = sums[:blocks] + sums[blocks:]
            for part in range(parts):
                row = part * blocks * slab_out + (s * per + c) * pieces + piece
                out_ref[pl.ds(row, blocks, stride=slab_out), :] = signals[:, part * LANES : (part + 1) * LANES]

    def signal(s, c):
        return [load_signal(s, c, part) for part in range(parts)]

    def channel(pair, c):
        one = pair[c * n1 : (c + 1) * n1]
        return jnp.concatenate([one] * parts, axis=0)

    t = outer_step([load_taps(c) for c in range(per)])
    m0 = outer_step(signal(0, 0))
    g0 = outer_step(signal(1, 0))
    t = inner_step(t)
    taps = [[channel(half, c) for half in t] for c in range(per)]
    m0 = inner_step(m0)
    m1 = outer_step(signal(0, 1))
    g0 = inner_step(g0)
    conv0 = back_inner_step(product(m0, taps[0]))
    g1 = outer_step(signal(1, 1))
    corr0 = back_inner_step(product_conjugate(g0, taps[0]))
    back_outer_step(0, 0, conv0)
    cross0 = back_inner_step(product_conjugate(g0, m0))
    m1 = inner_step(m1)
    back_outer_step(1, 0, corr0)
    back_outer_step(2, 0, cross0)
    g1 = inner_step(g1)
    conv1 = back_inner_step(product(m1, taps[1]))
    corr1 = back_inner_step(product_conjugate(g1, taps[1]))
    cross1 = back_inner_step(product_conjugate(g1, m1))
    back_outer_step(0, 1, conv1)
    back_outer_step(1, 1, corr1)
    back_outer_step(2, 1, cross1)


def params(size):
    return pltpu.CompilerParams(vmem_limit_bytes=size << 20)


def exchange(slabs, devices):
    slabs = slabs.reshape(devices, -1, 4, LANES)
    slabs = lax.all_to_all(slabs, ALL_AXES, split_axis=0, concat_axis=0, tiled=True)
    return slabs.reshape(-1, LANES)


def per_device(query_gate, key_gate, value_seq, grad_output, filter_taps):
    parts = lax.axis_size("dp")
    blocks = lax.axis_size(BLOCK_AXES)
    devices = parts * blocks
    rows, channels = query_gate.shape
    per = channels // devices
    pieces = rows // LANES
    operands = (key_gate, value_seq, grad_output, query_gate, filter_taps)
    in_hbm = pl.BlockSpec(memory_space=pltpu.HBM)
    in_vmem = pl.BlockSpec(memory_space=pltpu.VMEM)
    gate = pltpu.VMEM((rows, channels), jnp.bfloat16)

    packed = pl.pallas_call(
        functools.partial(pack_kernel, parts, devices),
        out_shape=jax.ShapeDtypeStruct((channels * (2 * pieces + pieces // parts), LANES), jnp.float32),
        in_specs=[in_hbm] * 5,
        out_specs=in_vmem,
        scratch_shapes=[gate] * 4
        + [pltpu.VMEM((rows // parts, channels), jnp.float32), pltpu.SemaphoreType.DMA((5,))],
        compiler_params=params(32),
        name="pack",
    )(*(pltpu.with_memory_space_constraint(x, pltpu.HBM) for x in operands))
    received = exchange(packed, devices)
    results = pl.pallas_call(
        functools.partial(convolve_kernel, parts, blocks, per),
        out_shape=jax.ShapeDtypeStruct((3 * channels * pieces, LANES), jnp.float32),
        compiler_params=params(48),
        name="convolve",
    )(received, *tables(blocks, rows))
    returned = exchange(results, devices)
    narrow = jax.ShapeDtypeStruct((rows, channels), jnp.bfloat16)
    wide = jax.ShapeDtypeStruct((rows, channels), jnp.float32)
    return pl.pallas_call(
        functools.partial(unpack_kernel, devices, 1.0 / math.sqrt(blocks * rows)),
        out_shape=(narrow, narrow, narrow, wide),
        in_specs=[in_vmem] * 4,
        out_specs=[in_hbm] * 4,
        scratch_shapes=[gate] * 3
        + [pltpu.VMEM((rows, channels), jnp.float32), pltpu.SemaphoreType.DMA((4, pieces))],
        compiler_params=params(32),
        name="unpack",
    )(returned, key_gate, value_seq, grad_output)


def solution(mesh):
    split_rows = P(ALL_AXES, None)
    return jax.shard_map(
        per_device,
        mesh=mesh,
        in_specs=(split_rows, split_rows, split_rows, split_rows, P(BLOCK_AXES, None)),
        out_specs=(split_rows, split_rows, split_rows, split_rows),
        check_vma=False,
    )
```
